32 devices in a mesh: ens: 8 (over z, y), mp: 4 (over x, core).
Axes of the slice: x: 2, y: 2, z: 4, core: 2. Of those that a mesh axis runs over, the one named last changes fastest.
Arguments:
- tokens: bfloat16 [8, 2048, 1024], P('ens', 'mp'), may hold values from -6 to 6
- ln_gain: float32 [1024], replicated, may hold values from 0.5 to 1.5
- w_qkv: bfloat16 [1024, 3072], replicated, may hold values from -1 to 1
- w_out: bfloat16 [1024, 1024], replicated, may hold values from -0.75 to 0.75
- neighbours: int32 [4, 8192], P(None, 'mp'), may hold values from 0 to 2047, as said below
- edge_weights: float32 [4, 8192], P(None, 'mp'), may hold values from 0.2 to 1
- w_dec: bfloat16 [100, 1024], replicated, may hold values from -0.1875 to 0.1875
- truth: float32 [100, 8192], P(None, ('mp', 'ens')), may hold values from -6 to 6
Outputs:
- crps_score: float32 [100, 8192], P(None, ('mp', 'ens'))
The draws below stay inside these ranges and needn't reach their ends.
Inputs may be any that keep to these rules, and one draw needn't show every extreme that they name: `neighbours`: the tokens of point g are among tokens g // 2048 * 512 to g // 2048 * 512 + 511 of its member.
All inputs are finite; a program needn't handle non-finite values.
Results may differ from the reference program's by a relative error of at most 0.0028.
The reference program's roundings to bfloat16 on the way (of `normed`, `projected`, `weights`, `context`, `processed`, `hidden` and `decoded`) count: a program that leaves them out, or rounds other values in their place, can miss the bound.
Values may be sent and summed in bfloat16 or wider, within the bound.
No kernel may reach another device: no remote copies, remote signals or barrier semaphores. Data moves between devices by JAX's collectives and lax.ppermute only.
A program may use at most 128 MiB of HBM per device.

```python
import jax
import jax.numpy as jnp
from jax import lax

D = 1024
HEADS = 16
VARS = 100
NEIGH = 4
HALF = 512
TOK_DEV = 512
GP_DEV = 2048
MEMBERS = 8
TOKENS = 2048
GRID = 8192
N_MP = 4


def draw_w_qkv(key, part):
    base = jax.random.normal(key, (D, 3 * D), jnp.float32) * D ** (-0.5)
    return jnp.clip(base, -1.0, 1.0).astype(jnp.bfloat16)


def draw_neighbours(key, part):
    block_first = jnp.arange(GRID, dtype=jnp.int32) // GP_DEV * TOK_DEV
    offsets = jax.random.randint(key, (NEIGH, GRID), 0, TOK_DEV, dtype=jnp.int32)
    result = block_first[None, :] + offsets
    result = result.at[0, 0].set(0)
    result = result.at[0, GRID - 1].set(TOKENS - 1)
    return result.astype(jnp.int32)


def level_of(rng, shape, pieces, least, top_value):
    gain = 1.0
    for dim, shards_of in pieces:
        draws = jax.random.uniform(jax.random.fold_in(jax.random.fold_in(rng, 6), dim), (shards_of,), jnp.float32, least / len(pieces), top_value / len(pieces))
        gain = gain * jnp.repeat(jnp.exp(draws), shape[dim] // shards_of).reshape((-1,) + (1,) * (len(shape) - 1 - dim))
    return gain


def gaussian(own_key, extent, width, reach, shards=(), held_as=jnp.bfloat16):
    factor_of = level_of(own_key, extent, shards, -0.22, 0.18) if shards else 1.0
    entries = jax.random.normal(own_key, extent, jnp.float32) * width * factor_of
    return jnp.minimum(jnp.maximum(entries, -reach), reach).astype(held_as)


def setup_inputs(seed: int = 0) -> dict:
    key_of = jax.random.split(jax.random.key(seed), 9)
    return {
        "tokens": gaussian(key_of[0], (MEMBERS, TOKENS, D), 1.0, 6.0, ((0, 8), (1, 4))),
        "ln_gain": jnp.clip(1.0 + 0.1 * jax.random.normal(key_of[1], (D,), jnp.float32), 0.5, 1.5),
        "w_qkv": draw_w_qkv(jax.random.fold_in(key_of[8], 71), 0),
        "w_out": gaussian(key_of[3], (D, D), (D // 16) ** -0.5, 0.75),
        "neighbours": draw_neighbours(jax.random.fold_in(key_of[8], 71), 0),
        "edge_weights": jnp.clip(0.2 + 0.8 * jax.random.uniform(key_of[5], (NEIGH, GRID), jnp.float32) ** level_of(key_of[5], (NEIGH, GRID), ((1, 4),), -0.2, 0.2), 0.2, 1.0),
        "w_dec": gaussian(key_of[6], (VARS, D), D ** -0.5, 0.1875),
        "truth": gaussian(key_of[7], (VARS, GRID), 1.0, 6.0, ((1, 32),), jnp.float32),
    }


ALPHA = 0.95

def layer_norm(inputs, ln_gain):
    values = inputs.astype(jnp.float32)
    average = lax.optimization_barrier(jnp.mean(values, axis=-1, keepdims=True))
    centred = values - average
    variance = lax.optimization_barrier(jnp.mean(centred * centred, axis=-1, keepdims=True))
    return (centred * lax.rsqrt(variance + 1e-05) * ln_gain).astype(jnp.bfloat16)

def attend(queries, key_rows, value_rows, first_row, seq_tokens):
    count = queries.shape[0]
    head_dim = queries.shape[-1]
    scores = jnp.einsum('qhe,khe->hqk', queries.astype(jnp.float32), key_rows.astype(jnp.float32)) / jnp.sqrt(jnp.float32(head_dim))
    query_pos = first_row + jnp.arange(count)
    key_pos = first_row - HALF + jnp.arange(count + 2 * HALF)
    allowed = (key_pos[None, :] >= 0) & (key_pos[None, :] < seq_tokens) & (jnp.abs(key_pos[None, :] - query_pos[:, None]) <= HALF)
    scores = jnp.where(allowed[None], scores, -1e+30)
    top = lax.optimization_barrier(jnp.max(scores, axis=-1, keepdims=True))
    expo = jnp.exp(scores - top)
    weights = (expo / lax.optimization_barrier(jnp.sum(expo, axis=-1, keepdims=True))).astype(jnp.bfloat16)
    context = jnp.einsum('hqk,khe->qhe', weights.astype(jnp.float32), value_rows.astype(jnp.float32))
    return context.astype(jnp.bfloat16)

def reference(tokens, ln_gain, w_qkv, w_out, neighbours, edge_weights, w_dec, truth):
    head_dim = D // HEADS

    def one_member(member_tokens):
        normed = layer_norm(member_tokens, ln_gain)
        projected = jnp.dot(normed, w_qkv, preferred_element_type=jnp.float32).astype(jnp.bfloat16)
        queries = projected[:, :D].reshape(TOKENS, HEADS, head_dim)
        key_rows = projected[:, D:2 * D].reshape(TOKENS, HEADS, head_dim)
        value_rows = projected[:, 2 * D:].reshape(TOKENS, HEADS, head_dim)
        key_pad = jnp.pad(key_rows, ((HALF, HALF), (0, 0), (0, 0)))
        value_pad = jnp.pad(value_rows, ((HALF, HALF), (0, 0), (0, 0)))

        def block_attend(block_index):
            first_row = block_index * TOK_DEV
            query_block = lax.dynamic_slice_in_dim(queries, first_row, TOK_DEV, 0)
            key_block = lax.dynamic_slice_in_dim(key_pad, first_row, TOK_DEV + 2 * HALF, 0)
            value_block = lax.dynamic_slice_in_dim(value_pad, first_row, TOK_DEV + 2 * HALF, 0)
            return attend(query_block, key_block, value_block, first_row, TOKENS)
        context = lax.map(block_attend, jnp.arange(N_MP, dtype=jnp.int32)).reshape(TOKENS, D)
        proj_out = jnp.dot(context, w_out, preferred_element_type=jnp.float32)
        processed = (member_tokens.astype(jnp.float32) + proj_out).astype(jnp.bfloat16)
        hidden = jnp.zeros((GRID, D), jnp.float32)
        for slot_index in range(NEIGH):
            picked = jnp.take(processed, neighbours[slot_index], axis=0)
            hidden = hidden + edge_weights[slot_index][:, None] * picked.astype(jnp.float32)
        decoded = jnp.dot(w_dec, hidden.astype(jnp.bfloat16).T, preferred_element_type=jnp.float32)
        return decoded.astype(jnp.bfloat16)
    decoded = lax.map(one_member, tokens).astype(jnp.float32)
    skill_term = lax.optimization_barrier(jnp.mean(jnp.abs(decoded - truth[None]), axis=0))
    spread = jnp.zeros_like(truth)
    for member_index in range(MEMBERS):
        spread = spread + lax.optimization_barrier(jnp.sum(jnp.abs(decoded[member_index][None] - decoded), axis=0))
    coeff = ALPHA / (2.0 * MEMBERS * (MEMBERS - 1)) + (1.0 - ALPHA) / (2.0 * MEMBERS * MEMBERS)
    return skill_term - coeff * spread
```

```python
import functools

import jax
import jax.numpy as jnp
from jax import lax
from jax.experimental import pallas as pl
from jax.experimental.pallas import tpu as pltpu
from jax.sharding import PartitionSpec as P

HEADS = 16
NEIGH = 4
HALF = 512
ALPHA = 0.95
EPS = 1e-05
MASKED = -1e30
GROUPS = 4
PAIR = 2

BF16 = jnp.bfloat16
F32 = jnp.float32
MIB = 1024 * 1024


def dot(a, b):
    return lax.dot_general(a, b, (((1,), (0,)), ((), ())), preferred_element_type=F32)


def dot_nt(a, b):
    return lax.dot_general(a, b, (((1,), (1,)), ((), ())), preferred_element_type=F32)


def layer_norm(inputs, ln_gain):
    values = inputs.astype(F32)
    average = jnp.mean(values, axis=-1, keepdims=True)
    centred = values - average
    variance = jnp.mean(centred * centred, axis=-1, keepdims=True)
    return (centred * lax.rsqrt(variance + EPS) * ln_gain).astype(BF16)


def halves(width):
    lane = lax.broadcasted_iota(jnp.int32, (1, width), 1)
    first = (lane < width // 2).astype(F32).astype(BF16)
    return first, (1.0 - first.astype(F32)).astype(BF16)


def value_side(values, masks):
    rows = values.shape[0]
    parts = []
    for mask in masks:
        ones = jnp.broadcast_to(mask, (rows, mask.shape[1]))
        parts.append(jnp.concatenate([values * mask, ones], axis=1))
    return jnp.concatenate(parts, axis=0)


def pair_attend(queries, keys, values_ext, masks, bias):
    width = queries.shape[1]
    tops, weights = [], []
    for mask in masks:
        scores = dot_nt(queries, keys * mask)
        if bias is not None:
            scores = scores + bias
        top = jnp.max(scores, axis=-1, keepdims=True)
        weights.append(jnp.exp(scores - top).astype(BF16))
        tops.append(top)
    both = dot(jnp.concatenate(weights, axis=1), values_ext)
    lane = lax.broadcasted_iota(jnp.int32, (queries.shape[0], width), 1)
    top = jnp.where(lane < width // 2, tops[0], tops[1])
    return both[:, :width], both[:, width:], top


def own_kernel(head_dim, x_ref, gain_ref, wq_ref, wk_ref, wv_ref, q_ref, sum_ref, total_ref, top_ref, normed_ref):
    @pl.when(pl.program_id(0) == 0)
    def _():
        normed_ref[...] = layer_norm(x_ref[...], gain_ref[...])

    rows, width = q_ref.shape
    normed = normed_ref[...]
    q_ref[...] = (dot(normed, wq_ref[...]).astype(BF16).astype(F32) * head_dim**-0.5).astype(BF16)
    keys = dot(normed, wk_ref[...]).astype(BF16)
    values = dot(normed, wv_ref[...]).astype(BF16)
    pair = PAIR * head_dim
    masks = halves(pair)
    step = rows // 2
    for first in range(0, width, pair):
        cols = slice(first, first + pair)
        values_ext = value_side(values[:, cols], masks)
        for row in range(0, rows, step):
            here = slice(row, row + step)
            sums, totals, top = pair_attend(q_ref[here, cols], keys[:, cols], values_ext, masks, None)
            sum_ref[here, cols] = sums
            total_ref[here, cols] = totals
            top_ref[here, cols] = top


def window_bias(rows, span, width, left_ok, right_ok, part):
    query = part * rows + lax.broadcasted_iota(jnp.int32, (rows, width), 0)
    key = part * rows + lax.broadcasted_iota(jnp.int32, (rows, width), 1)
    position = jnp.where(key < span, key - span, key)
    near = jnp.abs(position - query) <= HALF
    there = jnp.where(key < span, left_ok, right_ok) > 0
    return jnp.where(near & there, 0.0, MASKED).astype(F32)


def rest_kernel(
    head_dim, dests,
    place_ref, left_ref, right_ref, gain_ref, wk_ref, wv_ref, q_ref, sum_ref, total_ref, top_ref,
    x_ref, wout_ref, wdec_ref, near_ref, edge_ref,
    out_ref,
    normed_ref, bias_ref, proj_ref, high_ref, low_ref,
):
    group = pl.program_id(0)
    rows, width = q_ref.shape
    part_rows = rows // 2
    span = part_rows * 3

    @pl.when(group == 0)
    def _():
        normed_ref[:rows] = layer_norm(left_ref[...], gain_ref[...])
        normed_ref[rows:] = layer_norm(right_ref[...], gain_ref[...])
        for part in range(2):
            bias_ref[part] = window_bias(part_rows, rows, span, place_ref[0], place_ref[1], part)

    normed = normed_ref[...]
    keys = dot(normed, wk_ref[...]).astype(BF16)
    values = dot(normed, wv_ref[...]).astype(BF16)
    pair = PAIR * head_dim
    masks = halves(pair)
    context = [[], []]
    for first in range(0, width, pair):
        cols = slice(first, first + pair)
        for part in range(2):
            here = slice(part * part_rows, (part + 1) * part_rows)
            there = slice(part * part_rows, part * part_rows + span)
            sums, totals, top = pair_attend(
                q_ref[here, cols], keys[there, cols], value_side(values[there, cols], masks), masks, bias_ref[part]
            )
            own_top = top_ref[here, cols]
            best = jnp.maximum(top, own_top)
            scale, own_scale = jnp.exp(top - best), jnp.exp(own_top - best)
            sums = sums * scale + sum_ref[here, cols] * own_scale
            totals = totals * scale + total_ref[here, cols] * own_scale
            context[part].append((sums / totals).astype(BF16))
    context = jnp.concatenate([jnp.concatenate(c, axis=1) for c in context], axis=0)
    added = dot(context, wout_ref[...])

    @pl.when(group == 0)
    def _():
        proj_ref[...] = x_ref[...].astype(F32) + added

    @pl.when(group > 0)
    def _():
        proj_ref[...] += added

    points = near_ref.shape[1]
    token = lax.broadcasted_iota(jnp.int32, (rows, points), 0) + place_ref[2]
    matrix = jnp.zeros((rows, points), F32)
    for k in range(NEIGH):
        matrix += jnp.where(token == near_ref[k : k + 1], edge_ref[k : k + 1], 0.0)
    high = matrix.astype(BF16)
    high_ref[group] = high
    low_ref[group] = (matrix - high.astype(F32)).astype(BF16)

    @pl.when(group == pl.num_programs(0) - 1)
    def _():
        fields = dot_nt(wdec_ref[...], proj_ref[...].astype(BF16))
        tall = fields.shape[0]
        fields_high = fields.astype(BF16)
        fields_low = (fields - fields_high.astype(F32)).astype(BF16)
        both = jnp.concatenate([fields_high, fields_low], axis=0)
        variables, each = out_ref.shape[1:]
        for g in range(high_ref.shape[0]):
            product = dot(both, high_ref[g])
            decoded = product[:tall] + product[tall:] + dot(fields_high, low_ref[g])
            decoded = decoded.astype(BF16)
            for d in range(points // each):
                out_ref[g * (points // each) + d] = decoded[:variables, d * each : (d + 1) * each]


def score_kernel(members, coeff, fields_ref, truth_ref, out_ref):
    fields = [fields_ref[m].astype(F32) for m in range(members)]
    truth = truth_ref[...]
    skill = sum(jnp.abs(f - truth) for f in fields) / members
    spread = sum(jnp.abs(fields[j] - fields[k]) for j in range(members) for k in range(j))
    out_ref[...] = skill - (2.0 * coeff) * spread


def whole(shape):
    return pl.BlockSpec(shape, lambda g: (0,) * len(shape))


def columns(shape, offset=0):
    return pl.BlockSpec(shape, lambda g: (0, offset + g))


def one_member(tokens, left, right, ln_gain, w_qkv, w_out, near, edge_weights, w_dec, place, dests):
    rows, model = tokens.shape
    head_dim = model // HEADS
    width = model // GROUPS
    points = near.shape[1]
    tall = -(-w_dec.shape[0] // 16) * 16
    gain = ln_gain[None]
    wide = lambda dtype: jax.ShapeDtypeStruct((rows, model), dtype)
    block = columns((rows, width))
    weight = lambda k: columns((model, width), k * GROUPS)
    queries, sums, totals, tops = pl.pallas_call(
        functools.partial(own_kernel, head_dim),
        grid=(GROUPS,),
        in_specs=[whole((rows, model)), whole((1, model)), weight(0), weight(1), weight(2)],
        out_specs=[block] * 4,
        out_shape=[wide(BF16), wide(F32), wide(F32), wide(F32)],
        scratch_shapes=[pltpu.VMEM((rows, model), BF16)],
        compiler_params=pltpu.CompilerParams(vmem_limit_bytes=40 * MIB),
        cost_estimate=pl.CostEstimate(
            flops=2 * rows * model * 3 * model + 16 * rows * rows * model, bytes_accessed=14 * MIB, transcendentals=HEADS * rows * rows
        ),
        name="own_tokens",
    )(tokens, gain, w_qkv, w_qkv, w_qkv)
    per_step = points // GROUPS
    return pl.pallas_call(
        functools.partial(rest_kernel, head_dim, dests),
        grid=(GROUPS,),
        in_specs=[
            pl.BlockSpec(memory_space=pltpu.SMEM),
            whole((rows, model)), whole((rows, model)), whole((1, model)), weight(1), weight(2),
            block, block, block, block,
            whole((rows, model)),
            pl.BlockSpec((width, model), lambda g: (g, 0)),
            whole((tall, model)),
            columns((NEIGH, per_step)), columns((NEIGH, per_step)),
        ],
        out_specs=whole((dests, w_dec.shape[0], points // dests)),
        out_shape=jax.ShapeDtypeStruct((dests, w_dec.shape[0], points // dests), BF16),
        scratch_shapes=[
            pltpu.VMEM((2 * rows, model), BF16),
            pltpu.VMEM((2, rows // 2, rows // 2 * 3), F32),
            pltpu.VMEM((rows, model), F32),
            pltpu.VMEM((GROUPS, rows, per_step), BF16),
            pltpu.VMEM((GROUPS, rows, per_step), BF16),
        ],
        compiler_params=pltpu.CompilerParams(vmem_limit_bytes=56 * MIB),
        cost_estimate=pl.CostEstimate(
            flops=2 * rows * model * 5 * model + 24 * rows * rows * model, bytes_accessed=20 * MIB, transcendentals=2 * HEADS * rows * rows
        ),
        name="neighbour_tokens",
    )(
        place, left, right, gain, w_qkv, w_qkv, queries, sums, totals, tops, tokens, w_out,
        jnp.pad(w_dec, ((0, tall - w_dec.shape[0]), (0, 0))), near, edge_weights,
    )


def shards(tokens, ln_gain, w_qkv, w_out, neighbours, edge_weights, w_dec, truth):
    lanes = lax.axis_size("mp")
    lane = lax.axis_index("mp")
    dests = lax.axis_size("ens")
    up = [(i, i + 1) for i in range(lanes - 1)]
    down = [(j, i) for i, j in up]
    left = lax.ppermute(tokens, "mp", up)
    right = lax.ppermute(tokens, "mp", down)
    rows = tokens.shape[1]
    place = jnp.stack([lane > 0, lane < lanes - 1, lane * rows]).astype(jnp.int32)
    decoded = jnp.stack(
        [
            one_member(tokens[m], left[m], right[m], ln_gain, w_qkv, w_out, neighbours, edge_weights, w_dec, place, dests)
            for m in range(tokens.shape[0])
        ]
    )
    gathered = lax.all_to_all(decoded, "ens", split_axis=1, concat_axis=0, tiled=True)
    gathered = gathered.reshape((-1,) + gathered.shape[2:])
    members = gathered.shape[0]
    coeff = ALPHA / (2.0 * members * (members - 1)) + (1.0 - ALPHA) / (2.0 * members * members)
    return pl.pallas_call(
        functools.partial(score_kernel, members, coeff),
        out_shape=jax.ShapeDtypeStruct(truth.shape, F32),
        name="scores",
    )(gathered, truth)


def solution(mesh):
    in_specs = (
        P("ens", "mp", None),
        P(),
        P(),
        P(),
        P(None, "mp"),
        P(None, "mp"),
        P(),
        P(None, ("mp", "ens")),
    )
    out_specs = P(None, ("mp", "ens"))
    return jax.shard_map(shards, mesh=mesh, in_specs=in_specs, out_specs=out_specs, check_vma=False)
```

```python
import functools

import jax
import jax.numpy as jnp
from jax import lax
from jax.experimental import pallas as pl
from jax.experimental.pallas import tpu as pltpu
from jax.sharding import PartitionSpec as P

HEADS = 16
NEIGH = 4
HALF = 512
ALPHA = 0.95
EPS = 1e-05
MASKED = -1e30
STEP_COLS = 512
STEP_PAIRS = 2
OWN_ROWS = 256
FAR_ROWS = 128
EDGE_ROWS = 256
EDGE_COLS = 512

BF16 = jnp.bfloat16
F32 = jnp.float32
MIB = 1024 * 1024


def dot(a, b):
    return lax.dot_general(a, b, (((1,), (0,)), ((), ())), preferred_element_type=F32)


def dot_nt(a, b):
    return lax.dot_general(a, b, (((1,), (1,)), ((), ())), preferred_element_type=F32)


def layer_norm(inputs, ln_gain):
    values = inputs.astype(F32)
    average = jnp.mean(values, axis=-1, keepdims=True)
    centred = values - average
    variance = jnp.mean(centred * centred, axis=-1, keepdims=True)
    return (centred * lax.rsqrt(variance + EPS) * ln_gain).astype(BF16)


def halves(width):
    lane = lax.broadcasted_iota(jnp.int32, (1, width), 1)
    first = (lane < width // 2).astype(F32)
    return first.astype(BF16), (1.0 - first).astype(BF16)


def value_sides(values, masks):
    return [jnp.concatenate([values * mask, jnp.broadcast_to(mask, values.shape)], axis=1) for mask in masks]


def pair_attend(queries, key_sides, values_ext, bias):
    width = queries.shape[1]
    count = key_sides.shape[0] // 2
    both_scores = dot_nt(queries, key_sides)
    tops, weights = [], []
    for side in range(2):
        scores = both_scores[:, side * count : (side + 1) * count]
        if bias is not None:
            scores = scores + bias
        top = jnp.max(scores, axis=-1, keepdims=True)
        weights.append(jnp.exp(scores - top).astype(BF16))
        tops.append(top)
    both = dot(jnp.concatenate(weights, axis=1), values_ext)
    lane = lax.broadcasted_iota(jnp.int32, (queries.shape[0], width), 1)
    top = jnp.where(lane < width // 2, tops[0], tops[1])
    return both[:, :width], both[:, width:], top


def project_kernel(head_dim, x_ref, gain_ref, w_ref, kv_out_ref, q_ref, kv_ref, normed_ref):
    step = pl.program_id(0)
    model = x_ref.shape[1]
    q_steps = model // STEP_COLS

    @pl.when(step == 0)
    def _():
        normed_ref[...] = layer_norm(x_ref[...], gain_ref[...])

    made = dot(normed_ref[...], w_ref[...])

    @pl.when(step < q_steps)
    def _():
        cols = pl.ds(pl.multiple_of(step * STEP_COLS, STEP_COLS), STEP_COLS)
        q_ref[:, cols] = (made.astype(BF16).astype(F32) * head_dim**-0.5).astype(BF16)

    @pl.when(step >= q_steps)
    def _():
        cols = pl.ds(pl.multiple_of((step - q_steps) * STEP_COLS, STEP_COLS), STEP_COLS)
        rounded = made.astype(BF16)
        kv_ref[:, cols] = rounded
        kv_out_ref[...] = rounded


def edge_matrix(near, edge, high_ref, low_ref, cols):
    rows = high_ref.shape[0]
    points = near.shape[1]
    totals = []
    for k in range(NEIGH):
        total = jnp.zeros((1, points), F32)
        for j in range(NEIGH):
            total += jnp.where(near[j : j + 1] == near[k : k + 1], edge[j : j + 1], 0.0)
        totals.append(total)
    highs = [t.astype(BF16) for t in totals]
    lows = [(t - h.astype(F32)).astype(BF16) for t, h in zip(totals, highs)]
    shape = (EDGE_ROWS, points)
    token = lax.broadcasted_iota(jnp.int32, shape, 0).astype(F32).astype(BF16)
    for first in range(0, rows, EDGE_ROWS):
        high = jnp.zeros(shape, BF16)
        low = jnp.zeros(shape, BF16)
        for k in range(NEIGH):
            row = near[k : k + 1] - first
            row = jnp.where((row >= 0) & (row < EDGE_ROWS), row, -1).astype(F32).astype(BF16)
            hit = token == row
            high = jnp.where(hit, highs[k], high)
            low = jnp.where(hit, lows[k], low)
        high_ref[first : first + EDGE_ROWS, cols] = high
        low_ref[first : first + EDGE_ROWS, cols] = low


def own_kernel(
    head_dim, q_ref, kv_ref, near_ref, edge_ref, x_hbm, w_hbm, wout_hbm,
    sum_ref, total_ref, top_ref, high_ref, low_ref, x_ref, wkv_ref, wout_ref,
    sems,
):
    rows, model = q_ref.shape
    copies = [
        pltpu.make_async_copy(w_hbm.at[:, pl.ds(model, 2 * model)], wkv_ref, sems.at[0]),
        pltpu.make_async_copy(wout_hbm, wout_ref, sems.at[1]),
        pltpu.make_async_copy(x_hbm, x_ref, sems.at[2]),
    ]
    for copy in copies:
        copy.start()
    base = lax.axis_index("mp") * rows
    pair = 2 * head_dim
    masks = halves(pair)

    @pl.loop(0, model // (pair * STEP_PAIRS))
    def _(step):
        for p in range(STEP_PAIRS):
            first = (step * STEP_PAIRS + p) * pair
            cols = pl.ds(pl.multiple_of(first, pair), pair)
            keys = kv_ref[:, cols]
            values = kv_ref[:, pl.ds(pl.multiple_of(model + first, pair), pair)]
            key_sides = jnp.concatenate([keys * mask for mask in masks], axis=0)
            values_ext = jnp.concatenate(value_sides(values, masks), axis=0)
            for row in range(0, rows, OWN_ROWS):
                here = slice(row, row + OWN_ROWS)
                sums, totals, top = pair_attend(q_ref[here, cols], key_sides, values_ext, None)
                sum_ref[here, cols] = sums
                total_ref[here, cols] = totals
                top_ref[here, cols] = top

    for first in range(0, near_ref.shape[1], EDGE_COLS):
        cols = slice(first, first + EDGE_COLS)
        edge_matrix(near_ref[:, cols] - base, edge_ref[:, cols], high_ref, low_ref, cols)
    for copy in copies:
        copy.wait()


def window_bias(count, rows, span, left_ok, right_ok, first):
    query = first + lax.broadcasted_iota(jnp.int32, (count, span), 0)
    key = first + lax.broadcasted_iota(jnp.int32, (count, span), 1)
    position = jnp.where(key < rows, key - rows, key)
    near = jnp.abs(position - query) <= HALF
    there = jnp.where(key < rows, left_ok, right_ok) > 0
    return jnp.where(near & there, 0.0, MASKED).astype(F32)


def far_kernel(
    head_dim, chip_kv_hbm, far_hbm, gain_ref, q_ref, sum_ref, total_ref, top_ref, high_ref, low_ref, x_ref,
    wkv_ref, wout_ref, wdec_ref,
    out_ref,
    far_ref, kv_ref, bias_ref, context_ref, sems,
):
    rows, model = q_ref.shape
    lane = lax.axis_index("mp")
    lanes = lax.axis_size("mp")
    odd = lane % 2
    chip_at = pl.ds(pl.multiple_of((1 - odd) * rows, rows), rows)
    far_at = pl.ds(pl.multiple_of(odd * rows, rows), rows)
    far_copy = pltpu.make_async_copy(far_hbm, far_ref, sems.at[0])
    chip_copy = pltpu.make_async_copy(chip_kv_hbm, kv_ref.at[chip_at], sems.at[1])
    far_copy.start()
    chip_copy.start()
    span = rows + FAR_ROWS
    left_ok = (lane > 0).astype(jnp.int32)
    right_ok = (lane < lanes - 1).astype(jnp.int32)
    for part in range(rows // FAR_ROWS):
        bias_ref[part] = window_bias(FAR_ROWS, rows, span, left_ok, right_ok, part * FAR_ROWS)
    far_copy.wait()
    far_ref[...] = layer_norm(far_ref[...], gain_ref[...])
    normed = far_ref[...]
    for first in range(0, 2 * model, model):
        kv_ref[far_at, first : first + model] = dot(normed, wkv_ref[:, first : first + model]).astype(BF16)
    chip_copy.wait()
    pair = 2 * head_dim
    masks = halves(pair)

    @pl.loop(0, model // (pair * STEP_PAIRS))
    def _(step):
        for p in range(STEP_PAIRS):
            first = (step * STEP_PAIRS + p) * pair
            cols = pl.ds(pl.multiple_of(first, pair), pair)
            keys = kv_ref[:, cols]
            values = kv_ref[:, pl.ds(pl.multiple_of(model + first, pair), pair)]
            keys = [keys * mask for mask in masks]
            values = value_sides(values, masks)
            for part in range(rows // FAR_ROWS):
                here = slice(part * FAR_ROWS, (part + 1) * FAR_ROWS)
                there = slice(part * FAR_ROWS, part * FAR_ROWS + span)
                sums, totals, top = pair_attend(
                    q_ref[here, cols],
                    jnp.concatenate([k[there] for k in keys], axis=0),
                    jnp.concatenate([v[there] for v in values], axis=0),
                    bias_ref[part],
                )
                own_top = top_ref[here, cols]
                best = jnp.maximum(top, own_top)
                scale, own_scale = jnp.exp(top - best), jnp.exp(own_top - best)
                sums = sums * scale + sum_ref[here, cols] * own_scale
                totals = totals * scale + total_ref[here, cols] * own_scale
                context_ref[here, cols] = (sums / totals).astype(BF16)

    processed = (x_ref[...].astype(F32) + dot(context_ref[...], wout_ref[...])).astype(BF16)
    fields = dot_nt(wdec_ref[...], processed)
    variables, each = out_ref.shape[1:]
    tall = -(-variables // 16) * 16
    fields = jnp.concatenate([fields, jnp.zeros((tall - variables, rows), F32)], axis=0)
    fields_high = fields.astype(BF16)
    fields_low = (fields - fields_high.astype(F32)).astype(BF16)
    both = jnp.concatenate([fields_high, fields_low], axis=0)
    for d in range(out_ref.shape[0]):
        cols = slice(d * each, (d + 1) * each)
        product = dot(both, high_ref[:, cols])
        decoded = product[:tall] + product[tall:] + dot(fields_high, low_ref[:, cols])
        out_ref[d] = decoded[:variables].astype(BF16)


def score_kernel(members, coeff, fields_ref, truth_ref, out_ref):
    fields = [fields_ref[m].astype(F32) for m in range(members)]
    truth = truth_ref[...]
    skill = sum(jnp.abs(f - truth) for f in fields) / members
    spread = sum(jnp.abs(fields[j] - fields[k]) for j in range(members) for k in range(j))
    out_ref[...] = skill - (2.0 * coeff) * spread


IN_VMEM = pl.BlockSpec(memory_space=pltpu.VMEM)
ANYWHERE = pl.BlockSpec(memory_space=pl.ANY)


def held(value):
    return pltpu.with_memory_space_constraint(value, pltpu.VMEM)


def exchange(value, first, lanes):
    partner = list(range(lanes))
    for i in range(first, lanes - 1, 2):
        partner[i], partner[i + 1] = i + 1, i
    return lax.ppermute(value, "mp", list(enumerate(partner)))


def one_member(tokens, far, ln_gain, w_qkv, w_out, near, edge_weights, w_dec):
    rows, model = tokens.shape
    head_dim = model // HEADS
    points = near.shape[1]
    lanes = lax.axis_size("mp")
    dests = lax.axis_size("ens")
    gain = ln_gain[None]
    q_steps = model // STEP_COLS
    kv_out, queries, kv = pl.pallas_call(
        functools.partial(project_kernel, head_dim),
        grid=(3 * q_steps,),
        in_specs=[
            pl.BlockSpec((rows, model), lambda s: (0, 0)),
            pl.BlockSpec((1, model), lambda s: (0, 0)),
            pl.BlockSpec((model, STEP_COLS), lambda s: (0, s)),
        ],
        out_specs=[pl.BlockSpec((rows, STEP_COLS), lambda s: (0, jnp.maximum(s - q_steps, 0))), IN_VMEM, IN_VMEM],
        out_shape=[
            jax.ShapeDtypeStruct((rows, 2 * model), BF16),
            pltpu.VMEM((rows, model), BF16),
            pltpu.VMEM((rows, 2 * model), BF16),
        ],
        scratch_shapes=[pltpu.VMEM((rows, model), BF16)],
        compiler_params=pltpu.CompilerParams(vmem_limit_bytes=32 * MIB),
        cost_estimate=pl.CostEstimate(flops=6 * rows * model * model, bytes_accessed=10 * MIB, transcendentals=0),
        name="project",
    )(tokens, gain, w_qkv)
    chip_kv = exchange(kv_out, 0, lanes)
    wide = pltpu.VMEM((rows, model), F32)
    edges = pltpu.VMEM((rows, points), BF16)
    sums, totals, tops, high, low, x, wkv, wout = pl.pallas_call(
        functools.partial(own_kernel, head_dim),
        in_specs=[IN_VMEM] * 4 + [ANYWHERE] * 3,
        out_specs=[IN_VMEM] * 8,
        out_shape=[
            wide, wide, wide, edges, edges,
            pltpu.VMEM((rows, model), BF16), pltpu.VMEM((model, 2 * model), BF16), pltpu.VMEM((model, model), BF16),
        ],
        scratch_shapes=[pltpu.SemaphoreType.DMA((3,))],
        compiler_params=pltpu.CompilerParams(vmem_limit_bytes=24 * MIB),
        cost_estimate=pl.CostEstimate(
            flops=16 * rows * rows * model, bytes_accessed=10 * MIB, transcendentals=HEADS * rows * rows
        ),
        name="own_tokens",
    )(held(queries), held(kv), near, edge_weights, tokens, w_qkv, w_out)
    span = rows + FAR_ROWS
    return pl.pallas_call(
        functools.partial(far_kernel, head_dim),
        in_specs=[ANYWHERE] * 2 + [IN_VMEM] * 11,
        out_specs=IN_VMEM,
        out_shape=jax.ShapeDtypeStruct((dests, w_dec.shape[0], points // dests), BF16),
        scratch_shapes=[
            pltpu.VMEM((rows, model), BF16),
            pltpu.VMEM((2 * rows, 2 * model), BF16),
            pltpu.VMEM((rows // FAR_ROWS, FAR_ROWS, span), F32),
            pltpu.VMEM((rows, model), BF16),
            pltpu.SemaphoreType.DMA((2,)),
        ],
        compiler_params=pltpu.CompilerParams(vmem_limit_bytes=32 * MIB),
        cost_estimate=pl.CostEstimate(
            flops=2 * rows * model * 3 * model + 20 * rows * rows * model, bytes_accessed=8 * MIB, transcendentals=HEADS * rows * span
        ),
        name="neighbour_tokens",
    )(
        chip_kv, far, gain, held(queries), held(sums), held(totals), held(tops), held(high), held(low), held(x),
        held(wkv), held(wout), w_dec,
    )


def shards(tokens, ln_gain, w_qkv, w_out, neighbours, edge_weights, w_dec, truth):
    lanes = lax.axis_size("mp")
    far = exchange(tokens, 1, lanes)
    decoded = jnp.stack(
        [
            one_member(tokens[m], far[m], ln_gain, w_qkv, w_out, neighbours, edge_weights, w_dec)
            for m in range(tokens.shape[0])
        ]
    )
    gathered = lax.all_to_all(decoded, "ens", split_axis=1, concat_axis=0, tiled=True)
    gathered = gathered.reshape((-1,) + gathered.shape[2:])
    members = gathered.shape[0]
    coeff = ALPHA / (2.0 * members * (members - 1)) + (1.0 - ALPHA) / (2.0 * members * members)
    return pl.pallas_call(
        functools.partial(score_kernel, members, coeff),
        out_shape=jax.ShapeDtypeStruct(truth.shape, F32),
        name="scores",
    )(gathered, truth)


def solution(mesh):
    in_specs = (
        P("ens", "mp", None),
        P(),
        P(),
        P(),
        P(None, "mp"),
        P(None, "mp"),
        P(),
        P(None, ("mp", "ens")),
    )
    out_specs = P(None, ("mp", "ens"))
    return jax.shard_map(shards, mesh=mesh, in_specs=in_specs, out_specs=out_specs, check_vma=False)
```

```python
import functools

import jax
import jax.numpy as jnp
from jax import lax
from jax.experimental import pallas as pl
from jax.experimental.pallas import tpu as pltpu
from jax.sharding import PartitionSpec as P

HEADS = 16
NEIGH = 4
HALF = 512
ALPHA = 0.95
EPS = 1e-05
MASKED = -1e30
STEP_COLS = 1024
LN_ROWS = 128
STEP_PAIRS = 4
FULL_STEPS = 1
OWN_ROWS = 256
AHEAD = 1
LAG = 0
FAR_ROWS = 128
EDGE_ROWS = 256
EDGE_COLS = 512

BF16 = jnp.bfloat16
F32 = jnp.float32
MIB = 1024 * 1024
VMEM_LIMIT = 63 * MIB
LONG = pl.CostEstimate(flops=MIB * MIB, bytes_accessed=MIB, transcendentals=0)


def dot(a, b):
    return lax.dot_general(a, b, (((1,), (0,)), ((), ())), preferred_element_type=F32)


def dot_nt(a, b):
    return lax.dot_general(a, b, (((1,), (1,)), ((), ())), preferred_element_type=F32)


def layer_norm(inputs, ln_gain):
    values = inputs.astype(F32)
    average = jnp.mean(values, axis=-1, keepdims=True)
    centred = values - average
    variance = jnp.mean(centred * centred, axis=-1, keepdims=True)
    return (centred * lax.rsqrt(variance + EPS) * ln_gain).astype(BF16)


def halves(width):
    lane = lax.broadcasted_iota(jnp.int32, (1, width), 1)
    first = (lane < width // 2).astype(F32)
    return first.astype(BF16), (1.0 - first).astype(BF16)


def value_sides(values, masks):
    return [jnp.concatenate([values * mask, jnp.broadcast_to(mask, values.shape)], axis=1) for mask in masks]


def pair_weigh(scores, bias):
    count = scores.shape[1] // 2
    tops, weights = [], []
    for side in range(2):
        kept = scores[:, side * count : (side + 1) * count]
        if bias is not None:
            kept = kept + bias
        top = jnp.max(kept, axis=-1, keepdims=True)
        weights.append(jnp.exp(kept - top).astype(BF16))
        tops.append(top)
    return jnp.concatenate(weights, axis=1), tops


def pair_sums(weights, tops, values_ext):
    both = dot(weights, values_ext)
    width = both.shape[1] // 2
    lane = lax.broadcasted_iota(jnp.int32, (both.shape[0], width), 1)
    return both[:, :width], both[:, width:], jnp.where(lane < width // 2, tops[0], tops[1])


def in_turn(items, score, weigh, finish):
    scored, weighed = [], []
    for i in range(len(items) + AHEAD + LAG):
        if i < len(items):
            scored.append(score(items[i]))
        if AHEAD <= i < len(items) + AHEAD:
            weighed.append(weigh(items[i - AHEAD], scored[i - AHEAD]))
        if i >= AHEAD + LAG:
            finish(items[i - AHEAD - LAG], weighed[i - AHEAD - LAG])


def project_kernel(head_dim, x_hbm, w_hbm, gain_ref, q_hbm, kv_hbm, x_ref, w_ref, made_ref, x_sem, w_sems, out_sems):
    steps, rows, width = made_ref.shape
    model = x_ref.shape[1]
    q_steps = model // width
    x_copy = pltpu.make_async_copy(x_hbm, x_ref, x_sem)
    x_copy.start()
    ins, outs = [], []
    for step in range(steps):
        cols = pl.ds(step * width, width)
        target = q_hbm.at[:, cols] if step < q_steps else kv_hbm.at[:, pl.ds((step - q_steps) * width, width)]
        ins.append(pltpu.make_async_copy(w_hbm.at[:, cols], w_ref.at[step], w_sems.at[step]))
        outs.append(pltpu.make_async_copy(made_ref.at[step], target, out_sems.at[step]))
    for copy in ins:
        copy.start()
    x_copy.wait()
    for first in range(0, rows, LN_ROWS):
        here = slice(first, first + LN_ROWS)
        x_ref[here] = layer_norm(x_ref[here], gain_ref[...])
    for step in range(steps):
        ins[step].wait()
        made = dot(x_ref[...], w_ref[step]).astype(BF16)
        if step < q_steps:
            made = (made.astype(F32) * head_dim**-0.5).astype(BF16)
        made_ref[step] = made
        outs[step].start()
    for copy in outs:
        copy.wait()


def edge_matrix(near, edge, high_ref, low_ref):
    rows = high_ref.shape[0]
    points = near.shape[1]
    totals = []
    for k in range(NEIGH):
        total = jnp.zeros((1, points), F32)
        for j in range(NEIGH):
            total += jnp.where(near[j : j + 1] == near[k : k + 1], edge[j : j + 1], 0.0)
        totals.append(total)
    highs = [t.astype(BF16) for t in totals]
    lows = [(t - h.astype(F32)).astype(BF16) for t, h in zip(totals, highs)]
    shape = (EDGE_ROWS, points)
    token = lax.broadcasted_iota(jnp.int32, shape, 0).astype(F32).astype(BF16)
    for first in range(0, rows, EDGE_ROWS):
        high = jnp.zeros(shape, BF16)
        low = jnp.zeros(shape, BF16)
        for k in range(NEIGH):
            row = near[k : k + 1] - first
            row = jnp.where((row >= 0) & (row < EDGE_ROWS), row, -1).astype(F32).astype(BF16)
            hit = token == row
            high = jnp.where(hit, highs[k], high)
            low = jnp.where(hit, lows[k], low)
        high_ref[first : first + EDGE_ROWS] = high
        low_ref[first : first + EDGE_ROWS] = low


def own_kernel(head_dim, q_hbm, kv_hbm, *refs):
    out_hbms, (q_ref, k_ref, v_ref), out_refs, (in_sems, out_sems) = refs[:3], refs[3:6], refs[6:9], refs[9:]
    pairs, rows, width = q_ref.shape
    model = q_hbm.shape[1]
    skipped = model - pairs * width
    ins, outs = [], []
    for p in range(pairs):
        here, there = pl.ds(p * width, width), pl.ds(skipped + p * width, width)
        sources = (q_hbm.at[:, there], kv_hbm.at[:, there], kv_hbm.at[:, pl.ds(model + skipped + p * width, width)])
        ins.append(
            [
                pltpu.make_async_copy(source, target.at[p], in_sems.at[p, i])
                for i, (source, target) in enumerate(zip(sources, (q_ref, k_ref, v_ref)))
            ]
        )
        outs.append(
            [
                pltpu.make_async_copy(source.at[p], target.at[:, here], out_sems.at[p, i])
                for i, (source, target) in enumerate(zip(out_refs, out_hbms))
            ]
        )
    for group in ins:
        for copy in group:
            copy.start()
    masks = halves(width)
    sides = {}

    def score(item):
        p, row = item
        if row == 0:
            for copy in ins[p]:
                copy.wait()
            sides[p] = (
                jnp.concatenate([k_ref[p] * mask for mask in masks], axis=0),
                jnp.concatenate(value_sides(v_ref[p], masks), axis=0),
            )
        return dot_nt(q_ref[p, row : row + OWN_ROWS], sides[p][0])

    def finish(item, weighed):
        p, row = item
        for out_ref, made in zip(out_refs, pair_sums(*weighed, sides[p][1])):
            out_ref[p, row : row + OWN_ROWS] = made
        if row + OWN_ROWS == rows:
            for copy in outs[p]:
                copy.start()

    in_turn([(p, row) for p in range(pairs) for row in range(0, rows, OWN_ROWS)], score, lambda _, s: pair_weigh(s, None), finish)
    for group in outs:
        for copy in group:
            copy.wait()


def window_bias(count, rows, span, left_ok, right_ok, first):
    query = first + lax.broadcasted_iota(jnp.int32, (count, span), 0)
    key = first + lax.broadcasted_iota(jnp.int32, (count, span), 1)
    position = jnp.where(key < rows, key - rows, key)
    near = jnp.abs(position - query) <= HALF
    there = jnp.where(key < rows, left_ok, right_ok) > 0
    return jnp.where(near & there, 0.0, MASKED).astype(F32)


def far_kernel(
    head_dim, far_hbm, w_hbm, chip_kv_hbm, own_kv_hbm, q_hbm, sum_hbm, total_hbm, top_hbm, wout_hbm, x_hbm,
    gain_ref, wdec_ref, near_ref, edge_ref,
    out_ref,
    far_ref, w_ref, kv_ref, q_ref, sum_ref, total_ref, top_ref, wout_ref, x_ref, high_ref, low_ref,
    bias_ref, context_ref, sems, step_sems,
):
    rows, model = q_ref.shape
    lane = lax.axis_index("mp")
    lanes = lax.axis_size("mp")
    odd = lane % 2
    chip_at = pl.ds(pl.multiple_of((1 - odd) * 2 * rows, rows), rows)
    far_at = pl.ds(pl.multiple_of(odd * 2 * rows, rows), rows)
    own_at = pl.ds(rows, rows)
    pair = 2 * head_dim
    width = pair * STEP_PAIRS
    steps = model // width
    far_copy = pltpu.make_async_copy(far_hbm, far_ref, sems.at[0])
    last_copies = [
        pltpu.make_async_copy(wout_hbm, wout_ref, sems.at[1]),
        pltpu.make_async_copy(x_hbm, x_ref, sems.at[2]),
    ]
    weight_copies, step_copies = [], []
    for step in range(steps):
        cols = pl.ds(step * width, width)
        sides = [cols, pl.ds(model + step * width, width)]
        weights = [(w_hbm.at[:, pl.ds(model + s.start, width)], w_ref.at[:, s]) for s in sides]
        moves = [(chip_kv_hbm.at[:, s], kv_ref.at[chip_at, s]) for s in sides] + [(q_hbm.at[:, cols], q_ref.at[:, cols])]
        if step < FULL_STEPS:
            moves += [(own_kv_hbm.at[:, s], kv_ref.at[own_at, s]) for s in sides]
        else:
            kept = pl.ds((step - FULL_STEPS) * width, width)
            moves += [
                (a.at[:, kept], b.at[:, kept])
                for a, b in ((sum_hbm, sum_ref), (total_hbm, total_ref), (top_hbm, top_ref))
            ]
        made = [pltpu.make_async_copy(a, b, step_sems.at[step, i]) for i, (a, b) in enumerate(weights + moves)]
        weight_copies.append(made[:2])
        step_copies.append(made[2:])

    far_copy.start()
    for copy in weight_copies[0] + step_copies[0]:
        copy.start()
    span = rows + FAR_ROWS
    left_ok = (lane > 0).astype(jnp.int32)
    right_ok = (lane < lanes - 1).astype(jnp.int32)
    parts = rows // FAR_ROWS
    for part in range(parts):
        bias_ref[part] = window_bias(FAR_ROWS, rows, span, left_ok, right_ok, part * FAR_ROWS)
    for first in range(0, near_ref.shape[1], EDGE_COLS):
        cols = slice(first, first + EDGE_COLS)
        edge_matrix(near_ref[:, cols] - lane * rows, edge_ref[:, cols], high_ref.at[:, cols], low_ref.at[:, cols])
    far_copy.wait()
    for first in range(0, rows, LN_ROWS):
        here = slice(first, first + LN_ROWS)
        far_ref[here] = layer_norm(far_ref[here], gain_ref[...])

    masks = halves(pair)
    for step in range(steps):
        later = weight_copies[step + 1] + step_copies[step + 1] if step + 1 < steps else last_copies
        for side, copy in enumerate(weight_copies[step]):
            cols = slice(side * model + step * width, side * model + (step + 1) * width)
            copy.wait()
            kv_ref[far_at, cols] = dot(far_ref[...], w_ref[:, cols]).astype(BF16)
        for copy in step_copies[step]:
            copy.wait()
        for copy in later:
            copy.start()
        full = step < FULL_STEPS
        sides = {}

        def window(part, full=full):
            left, right = slice(part * FAR_ROWS, rows), slice(2 * rows, 2 * rows + (part + 1) * FAR_ROWS)
            return [slice(left.start, right.stop)] if full else [left, right]

        def score(item, sides=sides, window=window):
            first, part = item
            cols = slice(first, first + pair)
            if part == 0:
                sides[first] = (
                    [kv_ref[:, cols] * mask for mask in masks],
                    value_sides(kv_ref[:, model + first : model + first + pair], masks),
                )
            keys = [k[w] for k in sides[first][0] for w in window(part)]
            return dot_nt(q_ref[part * FAR_ROWS : (part + 1) * FAR_ROWS, cols], jnp.concatenate(keys, axis=0))

        def weigh(item, scores, full=full):
            part = item[1]
            bias = bias_ref[part]
            if full:
                reach = rows - part * FAR_ROWS
                bias = jnp.concatenate([bias[:, :reach], jnp.zeros((FAR_ROWS, rows), F32), bias[:, reach:]], axis=1)
            return pair_weigh(scores, bias)

        def finish(item, weighed, sides=sides, window=window, full=full):
            first, part = item
            here = slice(part * FAR_ROWS, (part + 1) * FAR_ROWS)
            values = [v[w] for v in sides[first][1] for w in window(part)]
            sums, totals, top = pair_sums(*weighed, jnp.concatenate(values, axis=0))
            if not full:
                kept = slice(first - FULL_STEPS * width, first - FULL_STEPS * width + pair)
                own_top = top_ref[here, kept]
                best = jnp.maximum(top, own_top)
                scale, own_scale = jnp.exp(top - best), jnp.exp(own_top - best)
                sums = sums * scale + sum_ref[here, kept] * own_scale
                totals = totals * scale + total_ref[here, kept] * own_scale
            context_ref[here, first : first + pair] = (sums / totals).astype(BF16)

        firsts = range(step * width, (step + 1) * width, pair)
        in_turn([(first, part) for first in firsts for part in range(parts)], score, weigh, finish)

    for copy in last_copies:
        copy.wait()
    processed = (x_ref[...].astype(F32) + dot(context_ref[...], wout_ref[...])).astype(BF16)
    fields = dot_nt(wdec_ref[...], processed)
    variables, each = out_ref.shape[1:]
    tall = -(-variables // 16) * 16
    fields = jnp.concatenate([fields, jnp.zeros((tall - variables, rows), F32)], axis=0)
    fields_high = fields.astype(BF16)
    fields_low = (fields - fields_high.astype(F32)).astype(BF16)
    both = jnp.concatenate([fields_high, fields_low], axis=0)
    for d in range(out_ref.shape[0]):
        cols = slice(d * each, (d + 1) * each)
        product = dot(both, high_ref[:, cols])
        decoded = product[:tall] + product[tall:] + dot(fields_high, low_ref[:, cols])
        out_ref[d] = decoded[:variables].astype(BF16)


def score_kernel(members, coeff, fields_ref, truth_ref, out_ref):
    fields = [fields_ref[m].astype(F32) for m in range(members)]
    truth = truth_ref[...]
    skill = sum(jnp.abs(f - truth) for f in fields) / members
    spread = sum(jnp.abs(fields[j] - fields[k]) for j in range(members) for k in range(j))
    out_ref[...] = skill - (2.0 * coeff) * spread


IN_VMEM = pl.BlockSpec(memory_space=pltpu.VMEM)
ANYWHERE = pl.BlockSpec(memory_space=pl.ANY)
IN_HBM = pl.BlockSpec(memory_space=pltpu.HBM)


def exchange(value, first, lanes):
    pairs = [(i, i + 1) for i in range(first, lanes - 1, 2)]
    return lax.ppermute(value, "mp", pairs + [(j, i) for i, j in pairs])


def project(tokens, gain, w_qkv):
    rows, model = tokens.shape
    steps = 3 * model // STEP_COLS
    return pl.pallas_call(
        functools.partial(project_kernel, model // HEADS),
        in_specs=[IN_HBM, IN_HBM, IN_VMEM],
        out_specs=[IN_HBM, IN_HBM],
        out_shape=[jax.ShapeDtypeStruct((rows, model), BF16), jax.ShapeDtypeStruct((rows, 2 * model), BF16)],
        scratch_shapes=[
            pltpu.VMEM((rows, model), BF16),
            pltpu.VMEM((steps, model, STEP_COLS), BF16),
            pltpu.VMEM((steps, rows, STEP_COLS), BF16),
            pltpu.SemaphoreType.DMA,
            pltpu.SemaphoreType.DMA((steps,)),
            pltpu.SemaphoreType.DMA((steps,)),
        ],
        compiler_params=pltpu.CompilerParams(vmem_limit_bytes=VMEM_LIMIT),
        cost_estimate=LONG,
        name="project",
    )(tokens, w_qkv, gain)


def own_attention(queries, kv):
    rows, model = queries.shape
    pair = 2 * model // HEADS
    pairs = HEADS // 2 - FULL_STEPS * STEP_PAIRS
    held = lambda dtype: pltpu.VMEM((pairs, rows, pair), dtype)
    return pl.pallas_call(
        functools.partial(own_kernel, model // HEADS),
        in_specs=[IN_HBM] * 2,
        out_specs=[IN_HBM] * 3,
        out_shape=[jax.ShapeDtypeStruct((rows, pairs * pair), F32)] * 3,
        scratch_shapes=[held(BF16)] * 3
        + [held(F32)] * 3
        + [pltpu.SemaphoreType.DMA((pairs, 3)), pltpu.SemaphoreType.DMA((pairs, 3))],
        compiler_params=pltpu.CompilerParams(vmem_limit_bytes=VMEM_LIMIT),
        cost_estimate=LONG,
        name="own_tokens",
    )(queries, kv)


def far_attention(
    far, w_qkv, chip_kv, own_kv, queries, sums, totals, tops, w_out, tokens, gain, w_dec, near, edge_weights, dests
):
    rows, model = tokens.shape
    points = near.shape[1]
    span = rows + FAR_ROWS
    steps = HEADS // (2 * STEP_PAIRS)
    held = lambda dtype, cols=model: pltpu.VMEM((rows, cols), dtype)
    return pl.pallas_call(
        functools.partial(far_kernel, model // HEADS),
        in_specs=[IN_HBM] * 10 + [IN_VMEM] * 4,
        out_specs=IN_VMEM,
        out_shape=jax.ShapeDtypeStruct((dests, w_dec.shape[0], points // dests), BF16),
        scratch_shapes=[
            held(BF16), pltpu.VMEM((model, 2 * model), BF16), pltpu.VMEM((3 * rows, 2 * model), BF16), held(BF16),
            held(F32, sums.shape[1]), held(F32, sums.shape[1]), held(F32, sums.shape[1]),
            pltpu.VMEM((model, model), BF16), held(BF16),
            held(BF16, points), held(BF16, points),
            pltpu.VMEM((rows // FAR_ROWS, FAR_ROWS, span), F32), held(BF16), pltpu.SemaphoreType.DMA((3,)),
            pltpu.SemaphoreType.DMA((steps, 8)),
        ],
        compiler_params=pltpu.CompilerParams(vmem_limit_bytes=VMEM_LIMIT),
        cost_estimate=LONG,
        name="neighbour_tokens",
    )(far, w_qkv, chip_kv, own_kv, queries, sums, totals, tops, w_out, tokens, gain, w_dec, near, edge_weights)


def one_member(tokens, far, ln_gain, w_qkv, w_out, near, edge_weights, w_dec):
    gain = ln_gain[None]
    queries, kv = project(tokens, gain, w_qkv)
    chip_kv = exchange(kv, 0, lax.axis_size("mp"))
    state = own_attention(queries, kv)
    return far_attention(
        far, w_qkv, chip_kv, kv, queries, *state, w_out, tokens, gain, w_dec, near, edge_weights, lax.axis_size("ens")
    )


def shards(tokens, ln_gain, w_qkv, w_out, neighbours, edge_weights, w_dec, truth):
    far = exchange(tokens, 1, lax.axis_size("mp"))
    decoded = jnp.stack(
        [
            one_member(tokens[m], far[m], ln_gain, w_qkv, w_out, neighbours, edge_weights, w_dec)
            for m in range(tokens.shape[0])
        ]
    )
    gathered = lax.all_to_all(decoded, "ens", split_axis=1, concat_axis=0, tiled=True)
    gathered = gathered.reshape((-1,) + gathered.shape[2:])
    members = gathered.shape[0]
    coeff = ALPHA / (2.0 * members * (members - 1)) + (1.0 - ALPHA) / (2.0 * members * members)
    return pl.pallas_call(
        functools.partial(score_kernel, members, coeff),
        out_shape=jax.ShapeDtypeStruct(truth.shape, F32),
        name="scores",
    )(gathered, truth)


def solution(mesh):
    in_specs = (
        P("ens", "mp", None),
        P(),
        P(),
        P(),
        P(None, "mp"),
        P(None, "mp"),
        P(),
        P(None, ("mp", "ens")),
    )
    out_specs = P(None, ("mp", "ens"))
    return jax.shard_map(shards, mesh=mesh, in_specs=in_specs, out_specs=out_specs, check_vma=False)
```

```python
import functools

import jax
import jax.numpy as jnp
from jax import lax
from jax.experimental import pallas as pl
from jax.experimental.pallas import tpu as pltpu
from jax.sharding import PartitionSpec as P

HEADS = 16
NEIGH = 4
HALF = 512
ALPHA = 0.95
EPS = 1e-05
MASKED = -1e30
STEP_COLS = 1024
LN_ROWS = 256
STEP_PAIRS = 4
FULL_STEPS = 1
OWN_ROWS = 128
AHEAD = 1
OWN_LAG = 1
FAR_LAG = 0
FAR_ROWS = 128
EDGE_ROWS = 256
EDGE_COLS = 512

BF16 = jnp.bfloat16
F32 = jnp.float32
MIB = 1024 * 1024
VMEM_LIMIT = 63 * MIB
LONG = pl.CostEstimate(flops=MIB * MIB, bytes_accessed=MIB, transcendentals=0)


def dot(a, b):
    return lax.dot_general(a, b, (((1,), (0,)), ((), ())), preferred_element_type=F32)


def dot_nt(a, b):
    return lax.dot_general(a, b, (((1,), (1,)), ((), ())), preferred_element_type=F32)


def layer_norm(inputs, ln_gain):
    values = inputs.astype(F32)
    average = jnp.mean(values, axis=-1, keepdims=True)
    centred = values - average
    variance = jnp.mean(centred * centred, axis=-1, keepdims=True)
    return (centred * lax.rsqrt(variance + EPS) * ln_gain).astype(BF16)


def halves(width):
    lane = lax.broadcasted_iota(jnp.int32, (1, width), 1)
    first = (lane < width // 2).astype(F32)
    return first.astype(BF16), (1.0 - first).astype(BF16)


def value_sides(values, masks):
    return [jnp.concatenate([values * mask, jnp.broadcast_to(mask, values.shape)], axis=1) for mask in masks]


def pair_weigh(scores, biases):
    count = scores.shape[1] // 2
    tops, weights = [], []
    for side in range(2):
        pieces, done = [], side * count
        for first, bias in biases:
            first += side * count
            if first > done:
                pieces.append(scores[:, done:first])
            done = first + bias.shape[1]
            pieces.append(scores[:, first:done] + bias)
        if done < (side + 1) * count:
            pieces.append(scores[:, done : (side + 1) * count])
        top = functools.reduce(jnp.maximum, [jnp.max(piece, axis=-1, keepdims=True) for piece in pieces])
        weights += [jnp.exp(piece - top).astype(BF16) for piece in pieces]
        tops.append(top)
    return jnp.concatenate(weights, axis=1), tops


def pair_sums(weights, tops, values_ext):
    both = dot(weights, values_ext)
    width = both.shape[1] // 2
    lane = lax.broadcasted_iota(jnp.int32, (both.shape[0], width), 1)
    return both[:, :width], both[:, width:], jnp.where(lane < width // 2, tops[0], tops[1])


def in_turn(items, lag, score, weigh, finish):
    scored, weighed = [], []
    for i in range(len(items) + AHEAD + lag):
        if i < len(items):
            scored.append(score(items[i]))
        if AHEAD <= i < len(items) + AHEAD:
            weighed.append(weigh(items[i - AHEAD], scored[i - AHEAD]))
        if i >= AHEAD + lag:
            finish(items[i - AHEAD - lag], weighed[i - AHEAD - lag])


def project_kernel(
    head_dim, x_hbm, w_hbm, gain_hbm, q_hbm, kv_hbm, x_ref, gain_ref, w_ref, made_ref, x_sem, gain_sem, w_sems, out_sems
):
    steps, rows, width = made_ref.shape
    model = x_ref.shape[1]
    q_steps = model // width
    x_copy = pltpu.make_async_copy(x_hbm, x_ref, x_sem)
    gain_copy = pltpu.make_async_copy(gain_hbm, gain_ref, gain_sem)
    gain_copy.start()
    x_copy.start()
    ins, outs = [], []
    for step in range(steps):
        cols = pl.ds(step * width, width)
        target = q_hbm.at[:, cols] if step < q_steps else kv_hbm.at[:, pl.ds((step - q_steps) * width, width)]
        ins.append(pltpu.make_async_copy(w_hbm.at[:, cols], w_ref.at[step], w_sems.at[step]))
        outs.append(pltpu.make_async_copy(made_ref.at[step], target, out_sems.at[step]))
    for copy in ins:
        copy.start()
    gain_copy.wait()
    x_copy.wait()
    for step in range(steps):
        ins[step].wait()
        part = LN_ROWS if step == 0 else rows
        for first in range(0, rows, part):
            here = slice(first, first + part)
            if step == 0:
                x_ref[here] = layer_norm(x_ref[here], gain_ref[...])
            made = dot(x_ref[here], w_ref[step]).astype(BF16)
            if step < q_steps:
                made = (made.astype(F32) * head_dim**-0.5).astype(BF16)
            made_ref[step, here] = made
        outs[step].start()
    for copy in outs:
        copy.wait()


def edge_matrix(near, edge, high_ref, low_ref):
    rows = high_ref.shape[0]
    points = near.shape[1]
    totals = []
    for k in range(NEIGH):
        total = jnp.zeros((1, points), F32)
        for j in range(NEIGH):
            total += jnp.where(near[j : j + 1] == near[k : k + 1], edge[j : j + 1], 0.0)
        totals.append(total)
    highs = [t.astype(BF16) for t in totals]
    lows = [(t - h.astype(F32)).astype(BF16) for t, h in zip(totals, highs)]
    shape = (EDGE_ROWS, points)
    token = lax.broadcasted_iota(jnp.int32, shape, 0).astype(F32).astype(BF16)
    for first in range(0, rows, EDGE_ROWS):
        high = jnp.zeros(shape, BF16)
        low = jnp.zeros(shape, BF16)
        for k in range(NEIGH):
            row = near[k : k + 1] - first
            row = jnp.where((row >= 0) & (row < EDGE_ROWS), row, -1).astype(F32).astype(BF16)
            hit = token == row
            high = jnp.where(hit, highs[k], high)
            low = jnp.where(hit, lows[k], low)
        high_ref[first : first + EDGE_ROWS] = high
        low_ref[first : first + EDGE_ROWS] = low


def own_kernel(head_dim, q_hbm, kv_hbm, *refs):
    out_hbms, (q_ref, k_ref, v_ref), out_refs, (in_sems, out_sems) = refs[:3], refs[3:6], refs[6:9], refs[9:]
    pairs, rows, width = q_ref.shape
    model = q_hbm.shape[1]
    skipped = model - pairs * width
    ins, outs = [], []
    for p in range(pairs):
        here, there = pl.ds(p * width, width), pl.ds(skipped + p * width, width)
        sources = (q_hbm.at[:, there], kv_hbm.at[:, there], kv_hbm.at[:, pl.ds(model + skipped + p * width, width)])
        ins.append(
            [
                pltpu.make_async_copy(source, target.at[p], in_sems.at[p, i])
                for i, (source, target) in enumerate(zip(sources, (q_ref, k_ref, v_ref)))
            ]
        )
        outs.append(
            [
                pltpu.make_async_copy(source.at[p], target.at[:, here], out_sems.at[p, i])
                for i, (source, target) in enumerate(zip(out_refs, out_hbms))
            ]
        )
    for group in ins:
        for copy in group:
            copy.start()
    masks = halves(width)
    sides = {}

    def score(item):
        p, row = item
        if row == 0:
            for copy in ins[p]:
                copy.wait()
            sides[p] = (
                jnp.concatenate([k_ref[p] * mask for mask in masks], axis=0),
                jnp.concatenate(value_sides(v_ref[p], masks), axis=0),
            )
        return dot_nt(q_ref[p, row : row + OWN_ROWS], sides[p][0])

    def finish(item, weighed):
        p, row = item
        for out_ref, made in zip(out_refs, pair_sums(*weighed, sides[p][1])):
            out_ref[p, row : row + OWN_ROWS] = made
        if row + OWN_ROWS == rows:
            for copy in outs[p]:
                copy.start()

    items = [(p, row) for p in range(pairs) for row in range(0, rows, OWN_ROWS)]
    in_turn(items, OWN_LAG, score, lambda _, s: pair_weigh(s, []), finish)
    for group in outs:
        for copy in group:
            copy.wait()


def window_bias(count, rows, span, left_ok, right_ok, first):
    query = first + lax.broadcasted_iota(jnp.int32, (count, span), 0)
    key = first + lax.broadcasted_iota(jnp.int32, (count, span), 1)
    position = jnp.where(key < rows, key - rows, key)
    near = jnp.abs(position - query) <= HALF
    there = jnp.where(key < rows, left_ok, right_ok) > 0
    return jnp.where(near & there, 0.0, MASKED).astype(F32)


def far_kernel(
    head_dim, far_hbm, w_hbm, chip_kv_hbm, own_kv_hbm, q_hbm, sum_hbm, total_hbm, top_hbm, wout_hbm, x_hbm,
    gain_hbm, wdec_hbm, near_hbm, edge_hbm,
    out_ref,
    gain_ref, wdec_ref, near_ref, edge_ref,
    far_ref, w_ref, kv_ref, q_ref, sum_ref, total_ref, top_ref, wout_ref, x_ref, high_ref, low_ref,
    bias_ref, context_ref, sems, step_sems,
):
    rows, model = q_ref.shape
    lane = lax.axis_index("mp")
    lanes = lax.axis_size("mp")
    odd = lane % 2
    chip_at = pl.ds(pl.multiple_of((1 - odd) * 2 * rows, rows), rows)
    far_at = pl.ds(pl.multiple_of(odd * 2 * rows, rows), rows)
    own_at = pl.ds(rows, rows)
    pair = 2 * head_dim
    width = pair * STEP_PAIRS
    steps = model // width
    far_copy = pltpu.make_async_copy(far_hbm, far_ref, sems.at[0])
    last_copies = [
        pltpu.make_async_copy(wout_hbm, wout_ref, sems.at[1]),
        pltpu.make_async_copy(x_hbm, x_ref, sems.at[2]),
        pltpu.make_async_copy(wdec_hbm, wdec_ref, sems.at[3]),
    ]
    gain_copy = pltpu.make_async_copy(gain_hbm, gain_ref, sems.at[4])
    edge_copies = [
        pltpu.make_async_copy(near_hbm, near_ref, sems.at[5]),
        pltpu.make_async_copy(edge_hbm, edge_ref, sems.at[6]),
    ]
    weight_copies, step_copies = [], []
    for step in range(steps):
        cols = pl.ds(step * width, width)
        sides = [cols, pl.ds(model + step * width, width)]
        weights = [(w_hbm.at[:, pl.ds(model + s.start, width)], w_ref.at[:, s]) for s in sides]
        moves = [(chip_kv_hbm.at[:, s], kv_ref.at[chip_at, s]) for s in sides] + [(q_hbm.at[:, cols], q_ref.at[:, cols])]
        if step < FULL_STEPS:
            moves += [(own_kv_hbm.at[:, s], kv_ref.at[own_at, s]) for s in sides]
        else:
            kept = pl.ds((step - FULL_STEPS) * width, width)
            moves += [
                (a.at[:, kept], b.at[:, kept])
                for a, b in ((sum_hbm, sum_ref), (total_hbm, total_ref), (top_hbm, top_ref))
            ]
        made = [pltpu.make_async_copy(a, b, step_sems.at[step, i]) for i, (a, b) in enumerate(weights + moves)]
        weight_copies.append(made[:2])
        step_copies.append(made[2:])

    for copy in edge_copies + [gain_copy, far_copy] + weight_copies[0] + step_copies[0]:
        copy.start()
    span = rows + FAR_ROWS
    left_ok = (lane > 0).astype(jnp.int32)
    right_ok = (lane < lanes - 1).astype(jnp.int32)
    parts = rows // FAR_ROWS
    for part in range(parts):
        bias_ref[part] = window_bias(FAR_ROWS, rows, span, left_ok, right_ok, part * FAR_ROWS)
    for copy in edge_copies:
        copy.wait()
    for first in range(0, near_ref.shape[1], EDGE_COLS):
        cols = slice(first, first + EDGE_COLS)
        edge_matrix(near_ref[:, cols] - lane * rows, edge_ref[:, cols], high_ref.at[:, cols], low_ref.at[:, cols])
    gain_copy.wait()
    far_copy.wait()
    for first in range(0, rows, LN_ROWS):
        here = slice(first, first + LN_ROWS)
        far_ref[here] = layer_norm(far_ref[here], gain_ref[...])

    masks = halves(pair)
    for step in range(steps):
        later = weight_copies[step + 1] + step_copies[step + 1] if step + 1 < steps else last_copies
        for side, copy in enumerate(weight_copies[step]):
            cols = slice(side * model + step * width, side * model + (step + 1) * width)
            copy.wait()
            kv_ref[far_at, cols] = dot(far_ref[...], w_ref[:, cols]).astype(BF16)
        for copy in step_copies[step]:
            copy.wait()
        for copy in later:
            copy.start()
        full = step < FULL_STEPS
        sides = {}

        def window(part, full=full):
            left, right = slice(part * FAR_ROWS, rows), slice(2 * rows, 2 * rows + (part + 1) * FAR_ROWS)
            return [slice(left.start, right.stop)] if full else [left, right]

        def score(item, sides=sides, window=window):
            first, part = item
            cols = slice(first, first + pair)
            if part == 0:
                sides[first] = (
                    [kv_ref[:, cols] * mask for mask in masks],
                    value_sides(kv_ref[:, model + first : model + first + pair], masks),
                )
            keys = [k[w] for k in sides[first][0] for w in window(part)]
            return dot_nt(q_ref[part * FAR_ROWS : (part + 1) * FAR_ROWS, cols], jnp.concatenate(keys, axis=0))

        def weigh(item, scores, full=full):
            part = item[1]
            bias = bias_ref[part]
            if full:
                reach = rows - part * FAR_ROWS
                return pair_weigh(scores, [(0, jnp.concatenate([bias[:, :reach], jnp.zeros((FAR_ROWS, rows), F32), bias[:, reach:]], axis=1))])
            return pair_weigh(scores, [(0, bias)])

        def finish(item, weighed, sides=sides, window=window, full=full):
            first, part = item
            here = slice(part * FAR_ROWS, (part + 1) * FAR_ROWS)
            values = [v[w] for v in sides[first][1] for w in window(part)]
            sums, totals, top = pair_sums(*weighed, jnp.concatenate(values, axis=0))
            if not full:
                kept = slice(first - FULL_STEPS * width, first - FULL_STEPS * width + pair)
                own_top = top_ref[here, kept]
                best = jnp.maximum(top, own_top)
                scale, own_scale = jnp.exp(top - best), jnp.exp(own_top - best)
                sums = sums * scale + sum_ref[here, kept] * own_scale
                totals = totals * scale + total_ref[here, kept] * own_scale
            context_ref[here, first : first + pair] = (sums / totals).astype(BF16)

        firsts = range(step * width, (step + 1) * width, pair)
        in_turn([(first, part) for first in firsts for part in range(parts)], FAR_LAG, score, weigh, finish)

    for copy in last_copies:
        copy.wait()
    processed = (x_ref[...].astype(F32) + dot(context_ref[...], wout_ref[...])).astype(BF16)
    fields = dot_nt(wdec_ref[...], processed)
    variables, each = out_ref.shape[1:]
    tall = -(-variables // 16) * 16
    fields = jnp.concatenate([fields, jnp.zeros((tall - variables, rows), F32)], axis=0)
    fields_high = fields.astype(BF16)
    fields_low = (fields - fields_high.astype(F32)).astype(BF16)
    both = jnp.concatenate([fields_high, fields_low], axis=0)
    for d in range(out_ref.shape[0]):
        cols = slice(d * each, (d + 1) * each)
        product = dot(both, high_ref[:, cols])
        decoded = product[:tall] + product[tall:] + dot(fields_high, low_ref[:, cols])
        out_ref[d] = decoded[:variables].astype(BF16)


def score_kernel(members, coeff, fields_ref, truth_ref, out_ref):
    fields = [fields_ref[m].astype(F32) for m in range(members)]
    truth = truth_ref[...]
    skill = sum(jnp.abs(f - truth) for f in fields) / members
    spread = sum(jnp.abs(fields[j] - fields[k]) for j in range(members) for k in range(j))
    out_ref[...] = skill - (2.0 * coeff) * spread


IN_VMEM = pl.BlockSpec(memory_space=pltpu.VMEM)
ANYWHERE = pl.BlockSpec(memory_space=pl.ANY)
IN_HBM = pl.BlockSpec(memory_space=pltpu.HBM)


def exchange(value, first, lanes):
    pairs = [(i, i + 1) for i in range(first, lanes - 1, 2)]
    return lax.ppermute(value, "mp", pairs + [(j, i) for i, j in pairs])


def project(tokens, gain, w_qkv):
    rows, model = tokens.shape
    steps = 3 * model // STEP_COLS
    return pl.pallas_call(
        functools.partial(project_kernel, model // HEADS),
        in_specs=[IN_HBM] * 3,
        out_specs=[IN_HBM, IN_HBM],
        out_shape=[jax.ShapeDtypeStruct((rows, model), BF16), jax.ShapeDtypeStruct((rows, 2 * model), BF16)],
        scratch_shapes=[
            pltpu.VMEM((rows, model), BF16),
            pltpu.VMEM((1, model), F32),
            pltpu.VMEM((steps, model, STEP_COLS), BF16),
            pltpu.VMEM((steps, rows, STEP_COLS), BF16),
            pltpu.SemaphoreType.DMA,
            pltpu.SemaphoreType.DMA,
            pltpu.SemaphoreType.DMA((steps,)),
            pltpu.SemaphoreType.DMA((steps,)),
        ],
        compiler_params=pltpu.CompilerParams(vmem_limit_bytes=VMEM_LIMIT),
        cost_estimate=LONG,
        name="project",
    )(tokens, w_qkv, gain)


def own_attention(queries, kv):
    rows, model = queries.shape
    pair = 2 * model // HEADS
    pairs = HEADS // 2 - FULL_STEPS * STEP_PAIRS
    held = lambda dtype: pltpu.VMEM((pairs, rows, pair), dtype)
    return pl.pallas_call(
        functools.partial(own_kernel, model // HEADS),
        in_specs=[IN_HBM] * 2,
        out_specs=[IN_HBM] * 3,
        out_shape=[jax.ShapeDtypeStruct((rows, pairs * pair), F32)] * 3,
        scratch_shapes=[held(BF16)] * 3
        + [held(F32)] * 3
        + [pltpu.SemaphoreType.DMA((pairs, 3)), pltpu.SemaphoreType.DMA((pairs, 3))],
        compiler_params=pltpu.CompilerParams(vmem_limit_bytes=VMEM_LIMIT),
        cost_estimate=LONG,
        name="own_tokens",
    )(queries, kv)


def far_attention(
    far, w_qkv, chip_kv, own_kv, queries, sums, totals, tops, w_out, tokens, gain, w_dec, near, edge_weights, dests
):
    rows, model = tokens.shape
    points = near.shape[1]
    span = rows + FAR_ROWS
    steps = HEADS // (2 * STEP_PAIRS)
    held = lambda dtype, cols=model: pltpu.VMEM((rows, cols), dtype)
    return pl.pallas_call(
        functools.partial(far_kernel, model // HEADS),
        in_specs=[IN_HBM] * 14,
        out_specs=IN_VMEM,
        out_shape=jax.ShapeDtypeStruct((dests, w_dec.shape[0], points // dests), BF16),
        scratch_shapes=[
            pltpu.VMEM((1, model), F32), pltpu.VMEM(w_dec.shape, BF16),
            pltpu.VMEM(near.shape, jnp.int32), pltpu.VMEM(near.shape, F32),
            held(BF16), pltpu.VMEM((model, 2 * model), BF16), pltpu.VMEM((3 * rows, 2 * model), BF16), held(BF16),
            held(F32, sums.shape[1]), held(F32, sums.shape[1]), held(F32, sums.shape[1]),
            pltpu.VMEM((model, model), BF16), held(BF16),
            held(BF16, points), held(BF16, points),
            pltpu.VMEM((rows // FAR_ROWS, FAR_ROWS, span), F32), held(BF16), pltpu.SemaphoreType.DMA((7,)),
            pltpu.SemaphoreType.DMA((steps, 8)),
        ],
        compiler_params=pltpu.CompilerParams(vmem_limit_bytes=VMEM_LIMIT),
        cost_estimate=LONG,
        name="neighbour_tokens",
    )(far, w_qkv, chip_kv, own_kv, queries, sums, totals, tops, w_out, tokens, gain, w_dec, near, edge_weights)


def one_member(tokens, far, ln_gain, w_qkv, w_out, near, edge_weights, w_dec):
    gain = ln_gain[None]
    queries, kv = project(tokens, gain, w_qkv)
    chip_kv = exchange(kv, 0, lax.axis_size("mp"))
    state = own_attention(queries, kv)
    return far_attention(
        far, w_qkv, chip_kv, kv, queries, *state, w_out, tokens, gain, w_dec, near, edge_weights, lax.axis_size("ens")
    )


def shards(tokens, ln_gain, w_qkv, w_out, neighbours, edge_weights, w_dec, truth):
    far = exchange(tokens, 1, lax.axis_size("mp"))
    decoded = jnp.stack(
        [
            one_member(tokens[m], far[m], ln_gain, w_qkv, w_out, neighbours, edge_weights, w_dec)
            for m in range(tokens.shape[0])
        ]
    )
    gathered = lax.all_to_all(decoded, "ens", split_axis=1, concat_axis=0, tiled=True)
    gathered = gathered.reshape((-1,) + gathered.shape[2:])
    members = gathered.shape[0]
    coeff = ALPHA / (2.0 * members * (members - 1)) + (1.0 - ALPHA) / (2.0 * members * members)
    return pl.pallas_call(
        functools.partial(score_kernel, members, coeff),
        out_shape=jax.ShapeDtypeStruct(truth.shape, F32),
        name="scores",
    )(gathered, truth)


def solution(mesh):
    in_specs = (
        P("ens", "mp", None),
        P(),
        P(),
        P(),
        P(None, "mp"),
        P(None, "mp"),
        P(),
        P(None, ("mp", "ens")),
    )
    out_specs = P(None, ("mp", "ens"))
    return jax.shard_map(shards, mesh=mesh, in_specs=in_specs, out_specs=out_specs, check_vma=False)
```

```python
import functools

import jax
import jax.numpy as jnp
from jax import lax
from jax.experimental import pallas as pl
from jax.experimental.pallas import tpu as pltpu
from jax.sharding import PartitionSpec as P

HEADS = 16
NEIGH = 4
HALF = 512
ALPHA = 0.95
EPS = 1e-05
MASKED = -1e30
STEP_COLS = 1024
LN_ROWS = 256
NORM_ROWS = 32
STEP_PAIRS = 4
LOOP_PAIRS = 2
FULL_STEPS = 1
OWN_ROWS = 128
AHEAD = 1
OWN_LAG = 1
FAR_LAG = 1
FAR_ROWS = 128
EDGE_ROWS = 256
EDGE_COLS = 512
EDGE_PART = 32
SCORE_ROWS = 16

BF16 = jnp.bfloat16
F32 = jnp.float32
MIB = 1024 * 1024
VMEM_LIMIT = 63 * MIB
SHARED_LIMIT = VMEM_LIMIT - 9 * MIB - MIB // 2
LONG = pl.CostEstimate(flops=MIB * MIB, bytes_accessed=MIB, transcendentals=0)


def dot(a, b):
    return lax.dot_general(a, b, (((1,), (0,)), ((), ())), preferred_element_type=F32)


def dot_nt(a, b):
    return lax.dot_general(a, b, (((1,), (1,)), ((), ())), preferred_element_type=F32)


def layer_norm(inputs, ln_gain):
    values = inputs.astype(F32)
    average = jnp.mean(values, axis=-1, keepdims=True)
    centred = values - average
    variance = jnp.mean(centred * centred, axis=-1, keepdims=True)
    return (centred * lax.rsqrt(variance + EPS) * ln_gain).astype(BF16)


def normalise(ref, here, ln_gain):
    for first in range(here.start, here.stop, NORM_ROWS):
        part = slice(first, first + NORM_ROWS)
        ref[part] = layer_norm(ref[part], ln_gain)


def halves(width):
    lane = lax.broadcasted_iota(jnp.int32, (1, width), 1)
    first = (lane < width // 2).astype(F32)
    return first.astype(BF16), (1.0 - first).astype(BF16)


def value_sides(values, masks):
    return [jnp.concatenate([values * mask, jnp.broadcast_to(mask, values.shape)], axis=1) for mask in masks]


def pair_weigh(scores, biases):
    count = scores.shape[1] // 2
    tops, weights = [], []
    for side in range(2):
        pieces, done = [], side * count
        for first, bias in biases:
            first += side * count
            if first > done:
                pieces.append(scores[:, done:first])
            done = first + bias.shape[1]
            pieces.append(scores[:, first:done] + bias)
        if done < (side + 1) * count:
            pieces.append(scores[:, done : (side + 1) * count])
        top = functools.reduce(jnp.maximum, [jnp.max(piece, axis=-1, keepdims=True) for piece in pieces])
        weights += [jnp.exp(piece - top).astype(BF16) for piece in pieces]
        tops.append(top)
    return jnp.concatenate(weights, axis=1), tops


def pair_sums(weights, tops, values_ext):
    both = dot(weights, values_ext)
    width = both.shape[1] // 2
    lane = lax.broadcasted_iota(jnp.int32, (both.shape[0], width), 1)
    return both[:, :width], both[:, width:], jnp.where(lane < width // 2, tops[0], tops[1])


def in_turn(items, lag, score, weigh, finish):
    scored, weighed = [], []
    for i in range(len(items) + AHEAD + lag):
        if i < len(items):
            scored.append(score(items[i]))
        if AHEAD <= i < len(items) + AHEAD:
            weighed.append(weigh(items[i - AHEAD], scored[i - AHEAD]))
        if i >= AHEAD + lag:
            finish(items[i - AHEAD - lag], weighed[i - AHEAD - lag])


def project_kernel(
    head_dim, x_hbm, w_hbm, gain_hbm, q_hbm, kv_hbm, x_ref, gain_ref, w_ref, made_ref, x_sem, gain_sem, w_sems, out_sems
):
    steps, rows, width = made_ref.shape
    model = x_ref.shape[1]
    q_steps = model // width
    x_copy = pltpu.make_async_copy(x_hbm, x_ref, x_sem)
    gain_copy = pltpu.make_async_copy(gain_hbm, gain_ref, gain_sem)
    gain_copy.start()
    x_copy.start()
    ins, outs = [], []
    for step in range(steps):
        cols = pl.ds(step * width, width)
        target = q_hbm.at[:, cols] if step < q_steps else kv_hbm.at[:, pl.ds((step - q_steps) * width, width)]
        ins.append(pltpu.make_async_copy(w_hbm.at[:, cols], w_ref.at[step], w_sems.at[step]))
        outs.append(pltpu.make_async_copy(made_ref.at[step], target, out_sems.at[step]))
    for copy in ins:
        copy.start()
    gain_copy.wait()
    x_copy.wait()
    for step in range(steps):
        ins[step].wait()
        part = LN_ROWS if step == 0 else rows
        for first in range(0, rows, part):
            here = slice(first, first + part)
            if step == 0:
                normalise(x_ref, here, gain_ref[...])
            made = dot(x_ref[here], w_ref[step]).astype(BF16)
            if step < q_steps:
                made = (made.astype(F32) * head_dim**-0.5).astype(BF16)
            made_ref[step, here] = made
        outs[step].start()
    for copy in outs:
        copy.wait()


def edge_matrix(near, edge, high_ref, low_ref):
    rows = high_ref.shape[0]
    points = near.shape[1]
    totals = []
    for k in range(NEIGH):
        total = jnp.zeros((1, points), F32)
        for j in range(NEIGH):
            total += jnp.where(near[j : j + 1] == near[k : k + 1], edge[j : j + 1], 0.0)
        totals.append(total)
    highs = [t.astype(BF16) for t in totals]
    lows = [(t - h.astype(F32)).astype(BF16) for t, h in zip(totals, highs)]
    shape = (EDGE_PART, points)
    for first in range(0, rows, EDGE_ROWS):
        near_rows = []
        for k in range(NEIGH):
            row = near[k : k + 1] - first
            near_rows.append(jnp.where((row >= 0) & (row < EDGE_ROWS), row, -1).astype(F32).astype(BF16))
        for part in range(0, EDGE_ROWS, EDGE_PART):
            token = (part + lax.broadcasted_iota(jnp.int32, shape, 0)).astype(F32).astype(BF16)
            high = jnp.zeros(shape, BF16)
            low = jnp.zeros(shape, BF16)
            for k in range(NEIGH):
                hit = token == near_rows[k]
                high = jnp.where(hit, highs[k], high)
                low = jnp.where(hit, lows[k], low)
            high_ref[first + part : first + part + EDGE_PART] = high
            low_ref[first + part : first + part + EDGE_PART] = low


def own_kernel(head_dim, q_hbm, kv_hbm, *refs):
    out_hbms, (q_ref, k_ref, v_ref), out_refs, (in_sems, out_sems) = refs[:3], refs[3:6], refs[6:9], refs[9:]
    pairs, rows, width = q_ref.shape
    model = q_hbm.shape[1]
    skipped = model - pairs * width
    ins, outs = [], []
    for p in range(pairs):
        here, there = pl.ds(p * width, width), pl.ds(skipped + p * width, width)
        sources = (q_hbm.at[:, there], kv_hbm.at[:, there], kv_hbm.at[:, pl.ds(model + skipped + p * width, width)])
        ins.append(
            [
                pltpu.make_async_copy(source, target.at[p], in_sems.at[p, i])
                for i, (source, target) in enumerate(zip(sources, (q_ref, k_ref, v_ref)))
            ]
        )
        outs.append(
            [
                pltpu.make_async_copy(source.at[p], target.at[:, here], out_sems.at[p, i])
                for i, (source, target) in enumerate(zip(out_refs, out_hbms))
            ]
        )
    for group in ins:
        for copy in group:
            copy.start()
    masks = halves(width)
    sides = {}

    def score(item):
        p, row = item
        if row == 0:
            for copy in ins[p]:
                copy.wait()
            sides[p] = (
                jnp.concatenate([k_ref[p] * mask for mask in masks], axis=0),
                jnp.concatenate(value_sides(v_ref[p], masks), axis=0),
            )
        return dot_nt(q_ref[p, row : row + OWN_ROWS], sides[p][0])

    def finish(item, weighed):
        p, row = item
        for out_ref, made in zip(out_refs, pair_sums(*weighed, sides[p][1])):
            out_ref[p, row : row + OWN_ROWS] = made
        if row + OWN_ROWS == rows:
            for copy in outs[p]:
                copy.start()

    items = [(p, row) for p in range(pairs) for row in range(0, rows, OWN_ROWS)]
    in_turn(items, OWN_LAG, score, lambda _, s: pair_weigh(s, []), finish)
    for group in outs:
        for copy in group:
            copy.wait()


def window_bias(count, rows, span, left_ok, right_ok, first):
    query = first + lax.broadcasted_iota(jnp.int32, (count, span), 0)
    key = first + lax.broadcasted_iota(jnp.int32, (count, span), 1)
    position = jnp.where(key < rows, key - rows, key)
    near = jnp.abs(position - query) <= HALF
    there = jnp.where(key < rows, left_ok, right_ok) > 0
    return jnp.where(near & there, 0.0, MASKED).astype(F32)


def far_kernel(
    head_dim, far_hbm, chip_kv_hbm, own_kv_hbm, q_hbm, sum_hbm, total_hbm, top_hbm,
    w_ref, wout_ref, x_ref, gain_ref, wdec_ref, near_ref, edge_ref,
    out_ref,
    far_ref, kv_ref, q_ref, sum_ref, total_ref, top_ref, high_ref, low_ref,
    bias_ref, context_ref, far_sem, step_sems,
):
    rows, model = q_ref.shape
    lane = lax.axis_index("mp")
    lanes = lax.axis_size("mp")
    odd = lane % 2
    chip_at = pl.ds(pl.multiple_of((1 - odd) * 2 * rows, rows), rows)
    far_at = pl.ds(pl.multiple_of(odd * 2 * rows, rows), rows)
    own_at = pl.ds(rows, rows)
    pair = 2 * head_dim
    width = pair * STEP_PAIRS
    steps = model // width
    far_copy = pltpu.make_async_copy(far_hbm, far_ref, far_sem)
    step_copies = []
    for step in range(steps):
        cols = pl.ds(step * width, width)
        sides = [cols, pl.ds(model + step * width, width)]
        moves = [(chip_kv_hbm.at[:, s], kv_ref.at[chip_at, s]) for s in sides] + [(q_hbm.at[:, cols], q_ref.at[:, cols])]
        if step < FULL_STEPS:
            moves += [(own_kv_hbm.at[:, s], kv_ref.at[own_at, s]) for s in sides]
        else:
            kept = pl.ds((step - FULL_STEPS) * width, width)
            moves += [
                (a.at[:, kept], b.at[:, kept])
                for a, b in ((sum_hbm, sum_ref), (total_hbm, total_ref), (top_hbm, top_ref))
            ]
        step_copies.append([pltpu.make_async_copy(a, b, step_sems.at[step, i]) for i, (a, b) in enumerate(moves)])

    for copy in [far_copy] + step_copies[0]:
        copy.start()
    span = rows + FAR_ROWS
    left_ok = (lane > 0).astype(jnp.int32)
    right_ok = (lane < lanes - 1).astype(jnp.int32)
    parts = rows // FAR_ROWS
    for part in range(parts):
        bias_ref[part] = window_bias(FAR_ROWS, rows, span, left_ok, right_ok, part * FAR_ROWS)
    for first in range(0, near_ref.shape[1], EDGE_COLS):
        cols = slice(first, first + EDGE_COLS)
        edge_matrix(near_ref[:, cols] - lane * rows, edge_ref[:, cols], high_ref.at[:, cols], low_ref.at[:, cols])
    far_copy.wait()
    for first in range(0, rows, LN_ROWS):
        here = slice(first, first + LN_ROWS)
        normalise(far_ref, here, gain_ref[...])

    masks = halves(pair)
    for step in range(steps):
        later = step_copies[step + 1] if step + 1 < steps else []
        for side in range(2):
            cols = slice(side * model + step * width, side * model + (step + 1) * width)
            kv_ref[far_at, cols] = dot(far_ref[...], w_ref[:, model + cols.start : model + cols.stop]).astype(BF16)
        for copy in step_copies[step]:
            copy.wait()
        for copy in later:
            copy.start()
        full = step < FULL_STEPS

        @pl.loop(0, STEP_PAIRS // LOOP_PAIRS)
        def _(turn, step=step, full=full):
            sides = {}

            def window(part):
                left, right = slice(part * FAR_ROWS, rows), slice(2 * rows, 2 * rows + (part + 1) * FAR_ROWS)
                return [slice(left.start, right.stop)] if full else [left, right]

            def columns(p, offset=0):
                first = offset + step * width + (turn * LOOP_PAIRS + p) * pair
                return pl.ds(pl.multiple_of(first, pair), pair)

            def score(item):
                p, part = item
                if part == 0:
                    sides[p] = (
                        [kv_ref[:, columns(p)] * mask for mask in masks],
                        value_sides(kv_ref[:, columns(p, model)], masks),
                    )
                keys = [k[w] for k in sides[p][0] for w in window(part)]
                queries = q_ref[part * FAR_ROWS : (part + 1) * FAR_ROWS, columns(p)]
                return dot_nt(queries, jnp.concatenate(keys, axis=0))

            def weigh(item, scores):
                bias = bias_ref[item[1]]
                if full:
                    reach = rows - item[1] * FAR_ROWS
                    bias = jnp.concatenate([bias[:, :reach], jnp.zeros((FAR_ROWS, rows), F32), bias[:, reach:]], axis=1)
                return pair_weigh(scores, [(0, bias)])

            def finish(item, weighed):
                p, part = item
                here = slice(part * FAR_ROWS, (part + 1) * FAR_ROWS)
                values = [v[w] for v in sides[p][1] for w in window(part)]
                sums, totals, top = pair_sums(*weighed, jnp.concatenate(values, axis=0))
                if not full:
                    kept = columns(p, -FULL_STEPS * width)
                    own_top = top_ref[here, kept]
                    best = jnp.maximum(top, own_top)
                    scale, own_scale = jnp.exp(top - best), jnp.exp(own_top - best)
                    sums = sums * scale + sum_ref[here, kept] * own_scale
                    totals = totals * scale + total_ref[here, kept] * own_scale
                context_ref[here, columns(p)] = (sums / totals).astype(BF16)

            in_turn([(p, part) for p in range(LOOP_PAIRS) for part in range(parts)], FAR_LAG, score, weigh, finish)

    processed = (x_ref[...].astype(F32) + dot(context_ref[...], wout_ref[...])).astype(BF16)
    fields = dot_nt(wdec_ref[...], processed)
    variables, each = out_ref.shape[1:]
    tall = -(-variables // 16) * 16
    fields = jnp.concatenate([fields, jnp.zeros((tall - variables, rows), F32)], axis=0)
    fields_high = fields.astype(BF16)
    fields_low = (fields - fields_high.astype(F32)).astype(BF16)
    both = jnp.concatenate([fields_high, fields_low], axis=0)
    for d in range(out_ref.shape[0]):
        cols = slice(d * each, (d + 1) * each)
        product = dot(both, high_ref[:, cols])
        decoded = product[:tall] + product[tall:] + dot(fields_high, low_ref[:, cols])
        out_ref[d] = decoded[:variables].astype(BF16)


def score_kernel(members, coeff, fields_ref, truth_ref, out_ref):
    rows = out_ref.shape[0]
    for first in range(0, rows, SCORE_ROWS):
        here = slice(first, min(first + SCORE_ROWS, rows))
        fields = [fields_ref[m, here].astype(F32) for m in range(members)]
        truth = truth_ref[here]
        skill = sum(jnp.abs(f - truth) for f in fields) / members
        spread = sum(jnp.abs(fields[j] - fields[k]) for j in range(members) for k in range(j))
        out_ref[here] = skill - (2.0 * coeff) * spread


IN_VMEM = pl.BlockSpec(memory_space=pltpu.VMEM)
ANYWHERE = pl.BlockSpec(memory_space=pl.ANY)
IN_HBM = pl.BlockSpec(memory_space=pltpu.HBM)


def near_by(value):
    return pltpu.with_memory_space_constraint(value, pltpu.VMEM)


def exchange(value, first, lanes):
    pairs = [(i, i + 1) for i in range(first, lanes - 1, 2)]
    return lax.ppermute(value, "mp", pairs + [(j, i) for i, j in pairs])


def project(tokens, gain, w_qkv):
    rows, model = tokens.shape
    steps = 3 * model // STEP_COLS
    return pl.pallas_call(
        functools.partial(project_kernel, model // HEADS),
        in_specs=[IN_HBM] * 3,
        out_specs=[IN_HBM, IN_HBM],
        out_shape=[jax.ShapeDtypeStruct((rows, model), BF16), jax.ShapeDtypeStruct((rows, 2 * model), BF16)],
        scratch_shapes=[
            pltpu.VMEM((rows, model), BF16),
            pltpu.VMEM((1, model), F32),
            pltpu.VMEM((steps, model, STEP_COLS), BF16),
            pltpu.VMEM((steps, rows, STEP_COLS), BF16),
            pltpu.SemaphoreType.DMA,
            pltpu.SemaphoreType.DMA,
            pltpu.SemaphoreType.DMA((steps,)),
            pltpu.SemaphoreType.DMA((steps,)),
        ],
        compiler_params=pltpu.CompilerParams(vmem_limit_bytes=VMEM_LIMIT),
        cost_estimate=LONG,
        name="project",
    )(tokens, w_qkv, gain)


def own_attention(queries, kv):
    rows, model = queries.shape
    pair = 2 * model // HEADS
    pairs = HEADS // 2 - FULL_STEPS * STEP_PAIRS
    held = lambda dtype: pltpu.VMEM((pairs, rows, pair), dtype)
    return pl.pallas_call(
        functools.partial(own_kernel, model // HEADS),
        in_specs=[IN_HBM] * 2,
        out_specs=[IN_HBM] * 3,
        out_shape=[jax.ShapeDtypeStruct((rows, pairs * pair), F32)] * 3,
        scratch_shapes=[held(BF16)] * 3
        + [held(F32)] * 3
        + [pltpu.SemaphoreType.DMA((pairs, 3)), pltpu.SemaphoreType.DMA((pairs, 3))],
        compiler_params=pltpu.CompilerParams(vmem_limit_bytes=SHARED_LIMIT),
        cost_estimate=LONG,
        name="own_tokens",
    )(queries, kv)


def far_attention(
    far, w_qkv, chip_kv, own_kv, queries, sums, totals, tops, w_out, tokens, gain, w_dec, near, edge_weights, dests
):
    rows, model = tokens.shape
    points = near.shape[1]
    span = rows + FAR_ROWS
    steps = HEADS // (2 * STEP_PAIRS)
    held = lambda dtype, cols=model: pltpu.VMEM((rows, cols), dtype)
    return pl.pallas_call(
        functools.partial(far_kernel, model // HEADS),
        in_specs=[IN_HBM] * 7 + [IN_VMEM] * 7,
        out_specs=IN_VMEM,
        out_shape=jax.ShapeDtypeStruct((dests, w_dec.shape[0], points // dests), BF16),
        scratch_shapes=[
            held(BF16), pltpu.VMEM((3 * rows, 2 * model), BF16), held(BF16),
            held(F32, sums.shape[1]), held(F32, sums.shape[1]), held(F32, sums.shape[1]),
            held(BF16, points), held(BF16, points),
            pltpu.VMEM((rows // FAR_ROWS, FAR_ROWS, span), F32), held(BF16), pltpu.SemaphoreType.DMA,
            pltpu.SemaphoreType.DMA((steps, 6)),
        ],
        compiler_params=pltpu.CompilerParams(vmem_limit_bytes=SHARED_LIMIT),
        cost_estimate=LONG,
        name="neighbour_tokens",
    )(
        far, chip_kv, own_kv, queries, sums, totals, tops,
        *[near_by(a) for a in (w_qkv, w_out, tokens, gain, w_dec, near, edge_weights)],
    )


def one_member(tokens, far, ln_gain, w_qkv, w_out, near, edge_weights, w_dec):
    gain = ln_gain[None]
    queries, kv = project(tokens, gain, w_qkv)
    chip_kv = exchange(kv, 0, lax.axis_size("mp"))
    state = own_attention(queries, kv)
    return far_attention(
        far, w_qkv, chip_kv, kv, queries, *state, w_out, tokens, gain, w_dec, near, edge_weights, lax.axis_size("ens")
    )


def shards(tokens, ln_gain, w_qkv, w_out, neighbours, edge_weights, w_dec, truth):
    far = exchange(tokens, 1, lax.axis_size("mp"))
    decoded = jnp.stack(
        [
            one_member(tokens[m], far[m], ln_gain, w_qkv, w_out, neighbours, edge_weights, w_dec)
            for m in range(tokens.shape[0])
        ]
    )
    gathered = lax.all_to_all(decoded, "ens", split_axis=1, concat_axis=0, tiled=True)
    gathered = gathered.reshape((-1,) + gathered.shape[2:])
    members = gathered.shape[0]
    coeff = ALPHA / (2.0 * members * (members - 1)) + (1.0 - ALPHA) / (2.0 * members * members)
    return pl.pallas_call(
        functools.partial(score_kernel, members, coeff),
        out_shape=jax.ShapeDtypeStruct(truth.shape, F32),
        name="scores",
    )(gathered, truth)


def solution(mesh):
    in_specs = (
        P("ens", "mp", None),
        P(),
        P(),
        P(),
        P(None, "mp"),
        P(None, "mp"),
        P(),
        P(None, ("mp", "ens")),
    )
    out_specs = P(None, ("mp", "ens"))
    return jax.shard_map(shards, mesh=mesh, in_specs=in_specs, out_specs=out_specs, check_vma=False)
```

```python
import functools

import jax
import jax.numpy as jnp
from jax import lax
from jax.experimental import pallas as pl
from jax.experimental.pallas import tpu as pltpu
from jax.sharding import PartitionSpec as P

HEADS = 16
NEIGH = 4
HALF = 512
ALPHA = 0.95
EPS = 1e-05
MASKED = -1e30
STEP_COLS = 1024
FAR_COLS = 1024
DECODE_COLS = 1024
LN_ROWS = 256
NORM_ROWS = 32
STEP_PAIRS = 4
LOOP_PAIRS = 4
FULL_STEPS = 1
OWN_ROWS = 128
AHEAD = 1
OWN_LAG = 1
FAR_AHEAD = 2
ONES_ROWS = 16
FAR_LAG = 3
FAR_ROWS = 128
EDGE_ROWS = 256
EDGE_COLS = 512
EDGE_PART = 32
SCORE_ROWS = 16

BF16 = jnp.bfloat16
F32 = jnp.float32
MIB = 1024 * 1024
VMEM_LIMIT = 63 * MIB
SHARED_LIMIT = VMEM_LIMIT - 9 * MIB - MIB // 2
LONG = pl.CostEstimate(flops=MIB * MIB, bytes_accessed=MIB, transcendentals=0)


def dot(a, b):
    return lax.dot_general(a, b, (((1,), (0,)), ((), ())), preferred_element_type=F32)


def dot_nt(a, b):
    return lax.dot_general(a, b, (((1,), (1,)), ((), ())), preferred_element_type=F32)


def layer_norm(inputs, ln_gain):
    values = inputs.astype(F32)
    average = jnp.mean(values, axis=-1, keepdims=True)
    centred = values - average
    variance = jnp.mean(centred * centred, axis=-1, keepdims=True)
    return (centred * lax.rsqrt(variance + EPS) * ln_gain).astype(BF16)


def normalise(ref, here, ln_gain):
    for first in range(here.start, here.stop, NORM_ROWS):
        part = slice(first, first + NORM_ROWS)
        ref[part] = layer_norm(ref[part], ln_gain)


def halves(width):
    lane = lax.broadcasted_iota(jnp.int32, (1, width), 1)
    first = (lane < width // 2).astype(F32)
    return first.astype(BF16), (1.0 - first).astype(BF16)


def value_sides(values, masks):
    return [jnp.concatenate([values * mask, jnp.broadcast_to(mask, values.shape)], axis=1) for mask in masks]


def pair_weigh(scores, biases):
    count = scores.shape[1] // 2
    tops, weights = [], []
    for side in range(2):
        pieces, done = [], side * count
        for first, bias in biases:
            first += side * count
            if first > done:
                pieces.append(scores[:, done:first])
            done = first + bias.shape[1]
            pieces.append(scores[:, first:done] + bias)
        if done < (side + 1) * count:
            pieces.append(scores[:, done : (side + 1) * count])
        top = functools.reduce(jnp.maximum, [jnp.max(piece, axis=-1, keepdims=True) for piece in pieces])
        weights += [jnp.exp(piece - top).astype(BF16) for piece in pieces]
        tops.append(top)
    return jnp.concatenate(weights, axis=1), tops


def pair_sums(weights, tops, values_ext):
    both = dot(weights, values_ext)
    width = both.shape[1] // 2
    lane = lax.broadcasted_iota(jnp.int32, (both.shape[0], width), 1)
    return both[:, :width], both[:, width:], jnp.where(lane < width // 2, tops[0], tops[1])


def tall_weigh(scores, biases):
    pieces, done = [], 0
    for first, bias in biases:
        if first > done:
            pieces.append(scores[done:first])
        done = first + bias.shape[0]
        pieces.append(scores[first:done] + bias)
    if done < scores.shape[0]:
        pieces.append(scores[done:])
    top = functools.reduce(jnp.maximum, [jnp.max(piece, axis=0, keepdims=True) for piece in pieces])
    return jnp.concatenate([jnp.exp(piece - top).astype(BF16) for piece in pieces], axis=0), top


def tall_sums(weights, top, values):
    width, count = values.shape[0], weights.shape[1] // 2
    ones = jnp.ones((ONES_ROWS, values.shape[1]), BF16)
    both = dot(jnp.concatenate([values, ones], axis=0), weights)
    both, total = both[:width], both[width : width + 1]
    first = lax.broadcasted_iota(jnp.int32, (width, count), 0) < width // 2
    return [jnp.where(first, a[:, :count], a[:, count:]) for a in (both, total, top)]


def in_turn(items, ahead, lag, score, weigh, finish):
    scored, weighed = [], []
    for i in range(len(items) + ahead + lag):
        if i < len(items):
            scored.append(score(items[i]))
        if ahead <= i < len(items) + ahead:
            weighed.append(weigh(items[i - ahead], scored[i - ahead]))
        if i >= ahead + lag:
            finish(items[i - ahead - lag], weighed[i - ahead - lag])


def project_kernel(
    head_dim, x_hbm, w_hbm, gain_hbm, q_hbm, kv_hbm, x_ref, gain_ref, w_ref, made_ref, x_sem, gain_sem, w_sems, out_sems
):
    steps, rows, width = made_ref.shape
    model = x_ref.shape[1]
    q_steps = model // width
    x_copy = pltpu.make_async_copy(x_hbm, x_ref, x_sem)
    gain_copy = pltpu.make_async_copy(gain_hbm, gain_ref, gain_sem)
    gain_copy.start()
    x_copy.start()
    ins, outs = [], []
    for step in range(steps):
        cols = pl.ds(step * width, width)
        target = q_hbm.at[:, cols] if step < q_steps else kv_hbm.at[:, pl.ds((step - q_steps) * width, width)]
        ins.append(pltpu.make_async_copy(w_hbm.at[:, cols], w_ref.at[step], w_sems.at[step]))
        outs.append(pltpu.make_async_copy(made_ref.at[step], target, out_sems.at[step]))
    for copy in ins:
        copy.start()
    gain_copy.wait()
    x_copy.wait()
    for step in range(steps):
        ins[step].wait()
        part = LN_ROWS if step == 0 else rows
        for first in range(0, rows, part):
            here = slice(first, first + part)
            if step == 0:
                normalise(x_ref, here, gain_ref[...])
            made = dot(x_ref[here], w_ref[step]).astype(BF16)
            if step < q_steps:
                made = (made.astype(F32) * head_dim**-0.5).astype(BF16)
            made_ref[step, here] = made
        outs[step].start()
    for copy in outs:
        copy.wait()


def edge_matrix(near, edge, high_ref, low_ref):
    rows = high_ref.shape[0]
    points = near.shape[1]
    totals = []
    for k in range(NEIGH):
        total = jnp.zeros((1, points), F32)
        for j in range(NEIGH):
            total += jnp.where(near[j : j + 1] == near[k : k + 1], edge[j : j + 1], 0.0)
        totals.append(total)
    highs = [t.astype(BF16) for t in totals]
    lows = [(t - h.astype(F32)).astype(BF16) for t, h in zip(totals, highs)]
    shape = (EDGE_PART, points)
    for first in range(0, rows, EDGE_ROWS):
        near_rows = []
        for k in range(NEIGH):
            row = near[k : k + 1] - first
            near_rows.append(jnp.where((row >= 0) & (row < EDGE_ROWS), row, -1).astype(F32).astype(BF16))
        for part in range(0, EDGE_ROWS, EDGE_PART):
            token = (part + lax.broadcasted_iota(jnp.int32, shape, 0)).astype(F32).astype(BF16)
            high = jnp.zeros(shape, BF16)
            low = jnp.zeros(shape, BF16)
            for k in range(NEIGH):
                hit = token == near_rows[k]
                high = jnp.where(hit, highs[k], high)
                low = jnp.where(hit, lows[k], low)
            high_ref[first + part : first + part + EDGE_PART] = high
            low_ref[first + part : first + part + EDGE_PART] = low


def own_kernel(head_dim, q_hbm, kv_hbm, *refs):
    out_hbms, (q_ref, k_ref, v_ref), out_refs, (in_sems, out_sems) = refs[:3], refs[3:6], refs[6:9], refs[9:]
    pairs, rows, width = q_ref.shape
    model = q_hbm.shape[1]
    skipped = model - pairs * width
    ins, outs = [], []
    for p in range(pairs):
        here, there = pl.ds(p * width, width), pl.ds(skipped + p * width, width)
        sources = (q_hbm.at[:, there], kv_hbm.at[:, there], kv_hbm.at[:, pl.ds(model + skipped + p * width, width)])
        ins.append(
            [
                pltpu.make_async_copy(source, target.at[p], in_sems.at[p, i])
                for i, (source, target) in enumerate(zip(sources, (q_ref, k_ref, v_ref)))
            ]
        )
        outs.append(
            [
                pltpu.make_async_copy(source.at[p], target.at[:, here], out_sems.at[p, i])
                for i, (source, target) in enumerate(zip(out_refs, out_hbms))
            ]
        )
    for group in ins:
        for copy in group:
            copy.start()
    masks = halves(width)
    sides = {}

    def score(item):
        p, row = item
        if row == 0:
            for copy in ins[p]:
                copy.wait()
            sides[p] = (
                jnp.concatenate([k_ref[p] * mask for mask in masks], axis=0),
                jnp.concatenate(value_sides(v_ref[p], masks), axis=0),
            )
        return dot_nt(q_ref[p, row : row + OWN_ROWS], sides[p][0])

    def finish(item, weighed):
        p, row = item
        for out_ref, made in zip(out_refs, pair_sums(*weighed, sides[p][1])):
            out_ref[p, row : row + OWN_ROWS] = made
        if row + OWN_ROWS == rows:
            for copy in outs[p]:
                copy.start()

    items = [(p, row) for p in range(pairs) for row in range(0, rows, OWN_ROWS)]
    in_turn(items, AHEAD, OWN_LAG, score, lambda _, s: pair_weigh(s, []), finish)
    for group in outs:
        for copy in group:
            copy.wait()


def window_bias(count, rows, span, left_ok, right_ok, first):
    key = first + lax.broadcasted_iota(jnp.int32, (span, 2 * count), 0)
    query = first + lax.broadcasted_iota(jnp.int32, (span, 2 * count), 1) % count
    position = jnp.where(key < rows, key - rows, key)
    near = jnp.abs(position - query) <= HALF
    there = jnp.where(key < rows, left_ok, right_ok) > 0
    return jnp.where(near & there, 0.0, MASKED).astype(F32)


def far_kernel(
    head_dim, far_hbm, chip_kv_hbm, own_kv_hbm, q_hbm, sum_hbm, total_hbm, top_hbm,
    w_ref, wout_ref, x_ref, gain_ref, wdec_ref, near_ref, edge_ref,
    out_ref,
    far_ref, kv_ref, q_ref, sum_ref, total_ref, top_ref, high_ref, low_ref,
    bias_ref, context_ref, far_sem, step_sems,
):
    rows, model = q_ref.shape
    lane = lax.axis_index("mp")
    lanes = lax.axis_size("mp")
    odd = lane % 2
    chip_at = pl.ds(pl.multiple_of((1 - odd) * 2 * rows, rows), rows)
    far_at = pl.ds(pl.multiple_of(odd * 2 * rows, rows), rows)
    own_at = pl.ds(rows, rows)
    pair = 2 * head_dim
    width = pair * STEP_PAIRS
    steps = model // width
    far_copy = pltpu.make_async_copy(far_hbm, far_ref, far_sem)
    step_copies = []
    for step in range(steps):
        cols = pl.ds(step * width, width)
        sides = [cols, pl.ds(model + step * width, width)]
        moves = [(chip_kv_hbm.at[:, s], kv_ref.at[chip_at, s]) for s in sides] + [(q_hbm.at[:, cols], q_ref.at[:, cols])]
        if step < FULL_STEPS:
            moves += [(own_kv_hbm.at[:, s], kv_ref.at[own_at, s]) for s in sides]
        else:
            kept = pl.ds((step - FULL_STEPS) * width, width)
            moves += [
                (a.at[:, kept], b.at[:, kept])
                for a, b in ((sum_hbm, sum_ref), (total_hbm, total_ref), (top_hbm, top_ref))
            ]
        step_copies.append([pltpu.make_async_copy(a, b, step_sems.at[step, i]) for i, (a, b) in enumerate(moves)])

    for copy in [far_copy] + step_copies[0]:
        copy.start()
    span = rows + FAR_ROWS
    left_ok = (lane > 0).astype(jnp.int32)
    right_ok = (lane < lanes - 1).astype(jnp.int32)
    parts = rows // FAR_ROWS
    for part in range(parts):
        bias_ref[part] = window_bias(FAR_ROWS, rows, span, left_ok, right_ok, part * FAR_ROWS)
    for first in range(0, near_ref.shape[1], EDGE_COLS):
        cols = slice(first, first + EDGE_COLS)
        edge_matrix(near_ref[:, cols] - lane * rows, edge_ref[:, cols], high_ref.at[:, cols], low_ref.at[:, cols])
    far_copy.wait()
    for first in range(0, rows, LN_ROWS):
        here = slice(first, first + LN_ROWS)
        normalise(far_ref, here, gain_ref[...])

    for first in range(0, 2 * model, FAR_COLS):
        cols = slice(first, first + FAR_COLS)
        kv_ref[far_at, cols] = dot(far_ref[...], w_ref[:, model + cols.start : model + cols.stop]).astype(BF16)

    masks = halves(pair)
    for step in range(steps):
        later = step_copies[step + 1] if step + 1 < steps else []
        for copy in step_copies[step]:
            copy.wait()
        for copy in later:
            copy.start()
        full = step < FULL_STEPS

        @pl.loop(0, STEP_PAIRS // LOOP_PAIRS)
        def _(turn, step=step, full=full):
            values = {}

            def window(part):
                left, right = slice(part * FAR_ROWS, rows), slice(2 * rows, 2 * rows + (part + 1) * FAR_ROWS)
                return [slice(left.start, right.stop)] if full else [left, right]

            def columns(p, offset=0):
                first = offset + step * width + (turn * LOOP_PAIRS + p) * pair
                return pl.ds(pl.multiple_of(first, pair), pair)

            def score(item):
                p, part = item
                if part == 0:
                    values[p] = kv_ref[:, columns(p, model)].T
                keys = jnp.concatenate([kv_ref[w, columns(p)] for w in window(part)], axis=0)
                queries = q_ref[part * FAR_ROWS : (part + 1) * FAR_ROWS, columns(p)]
                return dot_nt(keys, jnp.concatenate([queries * mask for mask in masks], axis=0))

            def weigh(item, scores):
                bias = bias_ref[item[1]]
                if full:
                    reach = rows - item[1] * FAR_ROWS
                    return tall_weigh(scores, [(0, bias[:reach]), (reach + rows, bias[reach:])])
                return tall_weigh(scores, [(0, bias)])

            def finish(item, weighed):
                p, part = item
                here = slice(part * FAR_ROWS, (part + 1) * FAR_ROWS)
                there = jnp.concatenate([values[p][:, w] for w in window(part)], axis=1)
                sums, totals, top = tall_sums(*weighed, there)
                if full:
                    context_ref[here, columns(p)] = (sums / totals).T.astype(BF16)
                    return
                sums, totals, top = sums.T, totals.T, top.T
                kept = columns(p, -FULL_STEPS * width)
                own_top = top_ref[here, kept]
                best = jnp.maximum(top, own_top)
                scale, own_scale = jnp.exp(top - best), jnp.exp(own_top - best)
                sums = sums * scale + sum_ref[here, kept] * own_scale
                totals = totals * scale + total_ref[here, kept] * own_scale
                context_ref[here, columns(p)] = (sums / totals).astype(BF16)

            in_turn([(p, part) for p in range(LOOP_PAIRS) for part in range(parts)], FAR_AHEAD, FAR_LAG, score, weigh, finish)

    processed = (x_ref[...].astype(F32) + dot(context_ref[...], wout_ref[...])).astype(BF16)
    fields = dot_nt(wdec_ref[...], processed)
    variables, each = out_ref.shape[1:]
    tall = -(-variables // 16) * 16
    fields = jnp.concatenate([fields, jnp.zeros((tall - variables, rows), F32)], axis=0)
    fields_high = fields.astype(BF16)
    fields_low = (fields - fields_high.astype(F32)).astype(BF16)
    both = jnp.concatenate([fields_high, fields_low], axis=0)
    points = high_ref.shape[1]
    for first in range(0, points, DECODE_COLS):
        cols = slice(first, first + DECODE_COLS)
        product = dot(both, high_ref[:, cols])
        decoded = product[:tall] + product[tall:] + dot(fields_high, low_ref[:, cols])
        decoded = decoded[:variables].astype(BF16)
        for at in range(0, DECODE_COLS, each):
            out_ref[(first + at) // each] = decoded[:, at : at + each]


def score_kernel(members, coeff, fields_ref, truth_ref, out_ref):
    rows = out_ref.shape[0]
    for first in range(0, rows, SCORE_ROWS):
        here = slice(first, min(first + SCORE_ROWS, rows))
        fields = [fields_ref[m, here].astype(F32) for m in range(members)]
        truth = truth_ref[here]
        skill = sum(jnp.abs(f - truth) for f in fields) / members
        spread = sum(jnp.abs(fields[j] - fields[k]) for j in range(members) for k in range(j))
        out_ref[here] = skill - (2.0 * coeff) * spread


IN_VMEM = pl.BlockSpec(memory_space=pltpu.VMEM)
ANYWHERE = pl.BlockSpec(memory_space=pl.ANY)
IN_HBM = pl.BlockSpec(memory_space=pltpu.HBM)


def near_by(value):
    return pltpu.with_memory_space_constraint(value, pltpu.VMEM)


def exchange(value, first, lanes):
    pairs = [(i, i + 1) for i in range(first, lanes - 1, 2)]
    return lax.ppermute(value, "mp", pairs + [(j, i) for i, j in pairs])


def project(tokens, gain, w_qkv):
    rows, model = tokens.shape
    steps = 3 * model // STEP_COLS
    return pl.pallas_call(
        functools.partial(project_kernel, model // HEADS),
        in_specs=[IN_HBM] * 3,
        out_specs=[IN_HBM, IN_HBM],
        out_shape=[jax.ShapeDtypeStruct((rows, model), BF16), jax.ShapeDtypeStruct((rows, 2 * model), BF16)],
        scratch_shapes=[
            pltpu.VMEM((rows, model), BF16),
            pltpu.VMEM((1, model), F32),
            pltpu.VMEM((steps, model, STEP_COLS), BF16),
            pltpu.VMEM((steps, rows, STEP_COLS), BF16),
            pltpu.SemaphoreType.DMA,
            pltpu.SemaphoreType.DMA,
            pltpu.SemaphoreType.DMA((steps,)),
            pltpu.SemaphoreType.DMA((steps,)),
        ],
        compiler_params=pltpu.CompilerParams(vmem_limit_bytes=VMEM_LIMIT),
        cost_estimate=LONG,
        name="project",
    )(tokens, w_qkv, gain)


def own_attention(queries, kv):
    rows, model = queries.shape
    pair = 2 * model // HEADS
    pairs = HEADS // 2 - FULL_STEPS * STEP_PAIRS
    held = lambda dtype: pltpu.VMEM((pairs, rows, pair), dtype)
    return pl.pallas_call(
        functools.partial(own_kernel, model // HEADS),
        in_specs=[IN_HBM] * 2,
        out_specs=[IN_HBM] * 3,
        out_shape=[jax.ShapeDtypeStruct((rows, pairs * pair), F32)] * 3,
        scratch_shapes=[held(BF16)] * 3
        + [held(F32)] * 3
        + [pltpu.SemaphoreType.DMA((pairs, 3)), pltpu.SemaphoreType.DMA((pairs, 3))],
        compiler_params=pltpu.CompilerParams(vmem_limit_bytes=SHARED_LIMIT),
        cost_estimate=LONG,
        name="own_tokens",
    )(queries, kv)


def far_attention(
    far, w_qkv, chip_kv, own_kv, queries, sums, totals, tops, w_out, tokens, gain, w_dec, near, edge_weights, dests
):
    rows, model = tokens.shape
    points = near.shape[1]
    span = rows + FAR_ROWS
    steps = HEADS // (2 * STEP_PAIRS)
    held = lambda dtype, cols=model: pltpu.VMEM((rows, cols), dtype)
    return pl.pallas_call(
        functools.partial(far_kernel, model // HEADS),
        in_specs=[IN_HBM] * 7 + [IN_VMEM] * 7,
        out_specs=IN_VMEM,
        out_shape=jax.ShapeDtypeStruct((dests, w_dec.shape[0], points // dests), BF16),
        scratch_shapes=[
            held(BF16), pltpu.VMEM((3 * rows, 2 * model), BF16), held(BF16),
            held(F32, sums.shape[1]), held(F32, sums.shape[1]), held(F32, sums.shape[1]),
            held(BF16, points), held(BF16, points),
            pltpu.VMEM((rows // FAR_ROWS, span, 2 * FAR_ROWS), F32), held(BF16), pltpu.SemaphoreType.DMA,
            pltpu.SemaphoreType.DMA((steps, 6)),
        ],
        compiler_params=pltpu.CompilerParams(vmem_limit_bytes=SHARED_LIMIT),
        cost_estimate=LONG,
        name="neighbour_tokens",
    )(
        far, chip_kv, own_kv, queries, sums, totals, tops,
        *[near_by(a) for a in (w_qkv, w_out, tokens, gain, w_dec, near, edge_weights)],
    )


def one_member(tokens, far, ln_gain, w_qkv, w_out, near, edge_weights, w_dec):
    gain = ln_gain[None]
    queries, kv = project(tokens, gain, w_qkv)
    chip_kv = exchange(kv, 0, lax.axis_size("mp"))
    state = own_attention(queries, kv)
    return far_attention(
        far, w_qkv, chip_kv, kv, queries, *state, w_out, tokens, gain, w_dec, near, edge_weights, lax.axis_size("ens")
    )


def shards(tokens, ln_gain, w_qkv, w_out, neighbours, edge_weights, w_dec, truth):
    far = exchange(tokens, 1, lax.axis_size("mp"))
    decoded = jnp.stack(
        [
            one_member(tokens[m], far[m], ln_gain, w_qkv, w_out, neighbours, edge_weights, w_dec)
            for m in range(tokens.shape[0])
        ]
    )
    gathered = lax.all_to_all(decoded, "ens", split_axis=1, concat_axis=0, tiled=True)
    gathered = gathered.reshape((-1,) + gathered.shape[2:])
    members = gathered.shape[0]
    coeff = ALPHA / (2.0 * members * (members - 1)) + (1.0 - ALPHA) / (2.0 * members * members)
    return pl.pallas_call(
        functools.partial(score_kernel, members, coeff),
        out_shape=jax.ShapeDtypeStruct(truth.shape, F32),
        name="scores",
    )(gathered, truth)


def solution(mesh):
    in_specs = (
        P("ens", "mp", None),
        P(),
        P(),
        P(),
        P(None, "mp"),
        P(None, "mp"),
        P(),
        P(None, ("mp", "ens")),
    )
    out_specs = P(None, ("mp", "ens"))
    return jax.shard_map(shards, mesh=mesh, in_specs=in_specs, out_specs=out_specs, check_vma=False)
```

```python
import functools

import jax
import jax.numpy as jnp
from jax import lax
from jax.experimental import pallas as pl
from jax.experimental.pallas import tpu as pltpu
from jax.sharding import PartitionSpec as P

HEADS = 16
NEIGH = 4
HALF = 512
ALPHA = 0.95
EPS = 1e-05
MASKED = -1e30
STEP_COLS = 1024
FAR_COLS = 1024
DECODE_COLS = 1024
LN_ROWS = 256
NORM_ROWS = 32
STEP_PAIRS = 4
LOOP_PAIRS = 4
FULL_STEPS = 1
OWN_ROWS = 128
AHEAD = 1
OWN_LAG = 1
FAR_AHEAD = 2
ONES_ROWS = 16
FAR_LAG = 3
FAR_ROWS = 128
EDGE_ROWS = 256
EDGE_COLS = 512
EDGE_PART = 32
SCORE_ROWS = 16

BF16 = jnp.bfloat16
F32 = jnp.float32
MIB = 1024 * 1024
VMEM_LIMIT = 63 * MIB
SHARED_LIMIT = VMEM_LIMIT - 9 * MIB - MIB // 2
LONG = pl.CostEstimate(flops=MIB * MIB, bytes_accessed=MIB, transcendentals=0)


def dot(a, b):
    return lax.dot_general(a, b, (((1,), (0,)), ((), ())), preferred_element_type=F32)


def dot_nt(a, b):
    return lax.dot_general(a, b, (((1,), (1,)), ((), ())), preferred_element_type=F32)


def layer_norm(inputs, ln_gain):
    values = inputs.astype(F32)
    average = jnp.mean(values, axis=-1, keepdims=True)
    centred = values - average
    variance = jnp.mean(centred * centred, axis=-1, keepdims=True)
    return (centred * lax.rsqrt(variance + EPS) * ln_gain).astype(BF16)


def normalise(ref, here, ln_gain):
    for first in range(here.start, here.stop, NORM_ROWS):
        part = slice(first, first + NORM_ROWS)
        ref[part] = layer_norm(ref[part], ln_gain)


def halves(width):
    lane = lax.broadcasted_iota(jnp.int32, (1, width), 1)
    first = (lane < width // 2).astype(F32)
    return first.astype(BF16), (1.0 - first).astype(BF16)


def value_sides(values, masks):
    return [jnp.concatenate([values * mask, jnp.broadcast_to(mask, values.shape)], axis=1) for mask in masks]


def pair_weigh(scores, biases):
    count = scores.shape[1] // 2
    tops, weights = [], []
    for side in range(2):
        pieces, done = [], side * count
        for first, bias in biases:
            first += side * count
            if first > done:
                pieces.append(scores[:, done:first])
            done = first + bias.shape[1]
            pieces.append(scores[:, first:done] + bias)
        if done < (side + 1) * count:
            pieces.append(scores[:, done : (side + 1) * count])
        top = functools.reduce(jnp.maximum, [jnp.max(piece, axis=-1, keepdims=True) for piece in pieces])
        weights += [jnp.exp(piece - top).astype(BF16) for piece in pieces]
        tops.append(top)
    return jnp.concatenate(weights, axis=1), tops


def pair_sums(weights, tops, values_ext):
    both = dot(weights, values_ext)
    width = both.shape[1] // 2
    lane = lax.broadcasted_iota(jnp.int32, (both.shape[0], width), 1)
    return both[:, :width], both[:, width:], jnp.where(lane < width // 2, tops[0], tops[1])


def tall_weigh(scores, biases):
    pieces, done = [], 0
    for first, bias in biases:
        if first > done:
            pieces.append(scores[done:first])
        done = first + bias.shape[0]
        pieces.append(scores[first:done] + bias)
    if done < scores.shape[0]:
        pieces.append(scores[done:])
    top = functools.reduce(jnp.maximum, [jnp.max(piece, axis=0, keepdims=True) for piece in pieces])
    return jnp.concatenate([jnp.exp(piece - top).astype(BF16) for piece in pieces], axis=0), top


def tall_sums(weights, top, values):
    width, count = values.shape[0], weights.shape[1] // 2
    ones = jnp.ones((ONES_ROWS, values.shape[1]), BF16)
    both = dot(jnp.concatenate([values, ones], axis=0), weights)
    both, total = both[:width], both[width : width + 1]
    first = lax.broadcasted_iota(jnp.int32, (width, count), 0) < width // 2
    return [jnp.where(first, a[:, :count], a[:, count:]) for a in (both, total, top)]


def in_turn(items, ahead, lag, score, weigh, finish):
    scored, weighed = [], []
    for i in range(len(items) + ahead + lag):
        if i < len(items):
            scored.append(score(items[i]))
        if ahead <= i < len(items) + ahead:
            weighed.append(weigh(items[i - ahead], scored[i - ahead]))
        if i >= ahead + lag:
            finish(items[i - ahead - lag], weighed[i - ahead - lag])


def project_kernel(
    head_dim, x_hbm, w_hbm, gain_hbm, q_hbm, kv_hbm, x_ref, gain_ref, w_ref, made_ref, x_sem, gain_sem, w_sems, out_sems
):
    steps, rows, width = made_ref.shape
    model = x_ref.shape[1]
    q_steps = model // width
    x_copy = pltpu.make_async_copy(x_hbm, x_ref, x_sem)
    gain_copy = pltpu.make_async_copy(gain_hbm, gain_ref, gain_sem)
    gain_copy.start()
    x_copy.start()
    ins, outs = [], []
    for step in range(steps):
        cols = pl.ds(step * width, width)
        target = q_hbm.at[:, cols] if step < q_steps else kv_hbm.at[:, pl.ds((step - q_steps) * width, width)]
        ins.append(pltpu.make_async_copy(w_hbm.at[:, cols], w_ref.at[step], w_sems.at[step]))
        outs.append(pltpu.make_async_copy(made_ref.at[step], target, out_sems.at[step]))
    for copy in ins:
        copy.start()
    gain_copy.wait()
    x_copy.wait()
    for step in range(steps):
        ins[step].wait()
        part = LN_ROWS if step == 0 else rows
        for first in range(0, rows, part):
            here = slice(first, first + part)
            if step == 0:
                normalise(x_ref, here, gain_ref[...])
            made = dot(x_ref[here], w_ref[step]).astype(BF16)
            if step < q_steps:
                made = (made.astype(F32) * head_dim**-0.5).astype(BF16)
            made_ref[step, here] = made
        outs[step].start()
    for copy in outs:
        copy.wait()


def edge_matrix(near, edge, high_ref, low_ref):
    rows = high_ref.shape[0]
    points = near.shape[1]
    totals = []
    for k in range(NEIGH):
        total = jnp.zeros((1, points), F32)
        for j in range(NEIGH):
            total += jnp.where(near[j : j + 1] == near[k : k + 1], edge[j : j + 1], 0.0)
        totals.append(total)
    highs = [t.astype(BF16) for t in totals]
    lows = [(t - h.astype(F32)).astype(BF16) for t, h in zip(totals, highs)]
    shape = (EDGE_PART, points)
    for first in range(0, rows, EDGE_ROWS):
        near_rows = []
        for k in range(NEIGH):
            row = near[k : k + 1] - first
            near_rows.append(jnp.where((row >= 0) & (row < EDGE_ROWS), row, -1).astype(F32).astype(BF16))
        for part in range(0, EDGE_ROWS, EDGE_PART):
            token = (part + lax.broadcasted_iota(jnp.int32, shape, 0)).astype(F32).astype(BF16)
            high = jnp.zeros(shape, BF16)
            low = jnp.zeros(shape, BF16)
            for k in range(NEIGH):
                hit = token == near_rows[k]
                high = jnp.where(hit, highs[k], high)
                low = jnp.where(hit, lows[k], low)
            high_ref[first + part : first + part + EDGE_PART] = high
            low_ref[first + part : first + part + EDGE_PART] = low


def own_kernel(head_dim, q_hbm, kv_hbm, *refs):
    out_hbms, (q_ref, k_ref, v_ref), out_refs, (in_sems, out_sems) = refs[:3], refs[3:6], refs[6:9], refs[9:]
    pairs, rows, width = q_ref.shape
    model = q_hbm.shape[1]
    skipped = model - pairs * width
    ins, outs = [], []
    for p in range(pairs):
        here, there = pl.ds(p * width, width), pl.ds(skipped + p * width, width)
        sources = (q_hbm.at[:, there], kv_hbm.at[:, there], kv_hbm.at[:, pl.ds(model + skipped + p * width, width)])
        ins.append(
            [
                pltpu.make_async_copy(source, target.at[p], in_sems.at[p, i])
                for i, (source, target) in enumerate(zip(sources, (q_ref, k_ref, v_ref)))
            ]
        )
        outs.append(
            [
                pltpu.make_async_copy(source.at[p], target.at[:, here], out_sems.at[p, i])
                for i, (source, target) in enumerate(zip(out_refs, out_hbms))
            ]
        )
    for group in ins:
        for copy in group:
            copy.start()
    masks = halves(width)
    sides = {}

    def score(item):
        p, row = item
        if row == 0:
            for copy in ins[p]:
                copy.wait()
            sides[p] = (
                jnp.concatenate([k_ref[p] * mask for mask in masks], axis=0),
                jnp.concatenate(value_sides(v_ref[p], masks), axis=0),
            )
        return dot_nt(q_ref[p, row : row + OWN_ROWS], sides[p][0])

    def finish(item, weighed):
        p, row = item
        for out_ref, made in zip(out_refs, pair_sums(*weighed, sides[p][1])):
            out_ref[p, row : row + OWN_ROWS] = made
        if row + OWN_ROWS == rows:
            for copy in outs[p]:
                copy.start()

    items = [(p, row) for p in range(pairs) for row in range(0, rows, OWN_ROWS)]
    in_turn(items, AHEAD, OWN_LAG, score, lambda _, s: pair_weigh(s, []), finish)
    for group in outs:
        for copy in group:
            copy.wait()


def window_bias(count, rows, span, left_ok, right_ok, first):
    key = first + lax.broadcasted_iota(jnp.int32, (span, 2 * count), 0)
    query = first + lax.broadcasted_iota(jnp.int32, (span, 2 * count), 1) % count
    position = jnp.where(key < rows, key - rows, key)
    near = jnp.abs(position - query) <= HALF
    there = jnp.where(key < rows, left_ok, right_ok) > 0
    return jnp.where(near & there, 0.0, MASKED).astype(F32)


def far_kernel(
    head_dim, far_hbm, chip_kv_hbm, own_kv_hbm, q_hbm, sum_hbm, total_hbm, top_hbm,
    w_ref, wout_ref, x_ref, gain_ref, wdec_ref, near_ref, edge_ref,
    out_ref,
    far_ref, kv_ref, q_ref, sum_ref, total_ref, top_ref, high_ref, low_ref,
    bias_ref, context_ref, far_sem, step_sems,
):
    rows, model = q_ref.shape
    lane = lax.axis_index("mp")
    lanes = lax.axis_size("mp")
    odd = lane % 2
    chip_at = pl.ds(pl.multiple_of((1 - odd) * 2 * rows, rows), rows)
    far_at = pl.ds(pl.multiple_of(odd * 2 * rows, rows), rows)
    own_at = pl.ds(rows, rows)
    pair = 2 * head_dim
    width = pair * STEP_PAIRS
    steps = model // width
    far_copy = pltpu.make_async_copy(far_hbm, far_ref, far_sem)
    step_copies = []
    for step in range(steps):
        cols = pl.ds(step * width, width)
        sides = [cols, pl.ds(model + step * width, width)]
        moves = [(chip_kv_hbm.at[:, s], kv_ref.at[chip_at, s]) for s in sides] + [(q_hbm.at[:, cols], q_ref.at[:, cols])]
        if step < FULL_STEPS:
            moves += [(own_kv_hbm.at[:, s], kv_ref.at[own_at, s]) for s in sides]
        else:
            kept = pl.ds((step - FULL_STEPS) * width, width)
            moves += [
                (a.at[:, kept], b.at[:, kept])
                for a, b in ((sum_hbm, sum_ref), (total_hbm, total_ref), (top_hbm, top_ref))
            ]
        step_copies.append([pltpu.make_async_copy(a, b, step_sems.at[step, i]) for i, (a, b) in enumerate(moves)])

    for copy in [far_copy] + step_copies[0]:
        copy.start()
    span = rows + FAR_ROWS
    left_ok = (lane > 0).astype(jnp.int32)
    right_ok = (lane < lanes - 1).astype(jnp.int32)
    parts = rows // FAR_ROWS
    for part in range(parts):
        bias_ref[part] = window_bias(FAR_ROWS, rows, span, left_ok, right_ok, part * FAR_ROWS)
    for first in range(0, near_ref.shape[1], EDGE_COLS):
        cols = slice(first, first + EDGE_COLS)
        edge_matrix(near_ref[:, cols] - lane * rows, edge_ref[:, cols], high_ref.at[:, cols], low_ref.at[:, cols])
    far_copy.wait()
    for first in range(0, rows, LN_ROWS):
        here = slice(first, first + LN_ROWS)
        normalise(far_ref, here, gain_ref[...])

    for first in range(0, 2 * model, FAR_COLS):
        cols = slice(first, first + FAR_COLS)
        kv_ref[far_at, cols] = dot(far_ref[...], w_ref[:, model + cols.start : model + cols.stop]).astype(BF16)

    masks = halves(pair)
    for step in range(steps):
        later = step_copies[step + 1] if step + 1 < steps else []
        for copy in step_copies[step]:
            copy.wait()
        for copy in later:
            copy.start()
        full = step < FULL_STEPS

        @pl.loop(0, STEP_PAIRS // LOOP_PAIRS)
        def _(turn, step=step, full=full):
            values = {}

            def window(part):
                left, right = slice(part * FAR_ROWS, rows), slice(2 * rows, 2 * rows + (part + 1) * FAR_ROWS)
                return [slice(left.start, right.stop)] if full else [left, right]

            def columns(p, offset=0):
                first = offset + step * width + (turn * LOOP_PAIRS + p) * pair
                return pl.ds(pl.multiple_of(first, pair), pair)

            def score(item):
                p, part = item
                if part == 0:
                    values[p] = kv_ref[:, columns(p, model)].T
                keys = jnp.concatenate([kv_ref[w, columns(p)] for w in window(part)], axis=0)
                queries = q_ref[part * FAR_ROWS : (part + 1) * FAR_ROWS, columns(p)]
                return dot_nt(keys, jnp.concatenate([queries * mask for mask in masks], axis=0))

            def weigh(item, scores):
                bias = bias_ref[item[1]]
                if full:
                    reach = rows - item[1] * FAR_ROWS
                    return tall_weigh(scores, [(0, bias[:reach]), (reach + rows, bias[reach:])])
                return tall_weigh(scores, [(0, bias)])

            def finish(item, weighed):
                p, part = item
                here = slice(part * FAR_ROWS, (part + 1) * FAR_ROWS)
                there = jnp.concatenate([values[p][:, w] for w in window(part)], axis=1)
                sums, totals, top = tall_sums(*weighed, there)
                if full:
                    context_ref[here, columns(p)] = (sums / totals).T.astype(BF16)
                    return
                sums, totals, top = sums.T, totals.T, top.T
                kept = columns(p, -FULL_STEPS * width)
                own_top = top_ref[here, kept]
                best = jnp.maximum(top, own_top)
                scale, own_scale = jnp.exp(top - best), jnp.exp(own_top - best)
                sums = sums * scale + sum_ref[here, kept] * own_scale
                totals = totals * scale + total_ref[here, kept] * own_scale
                context_ref[here, columns(p)] = (sums / totals).astype(BF16)

            in_turn([(p, part) for p in range(LOOP_PAIRS) for part in range(parts)], FAR_AHEAD, FAR_LAG, score, weigh, finish)

    processed = (x_ref[...].astype(F32) + dot(context_ref[...], wout_ref[...])).astype(BF16)
    fields = dot_nt(wdec_ref[...], processed)
    variables, each = out_ref.shape[1:]
    tall = -(-variables // 16) * 16
    fields = jnp.concatenate([fields, jnp.zeros((tall - variables, rows), F32)], axis=0)
    fields_high = fields.astype(BF16)
    fields_low = (fields - fields_high.astype(F32)).astype(BF16)
    both = jnp.concatenate([fields_high, fields_low], axis=0)
    points = high_ref.shape[1]
    for first in range(0, points, DECODE_COLS):
        cols = slice(first, first + DECODE_COLS)
        product = dot(both, high_ref[:, cols])
        decoded = product[:tall] + product[tall:] + dot(fields_high, low_ref[:, cols])
        decoded = decoded[:variables].astype(BF16)
        for at in range(0, DECODE_COLS, each):
            out_ref[(first + at) // each] = decoded[:, at : at + each]


def score_kernel(members, coeff, fields_ref, truth_ref, out_ref):
    rows = out_ref.shape[0]
    for first in range(0, rows, SCORE_ROWS):
        here = slice(first, min(first + SCORE_ROWS, rows))
        fields = [fields_ref[m, here].astype(F32) for m in range(members)]
        truth = truth_ref[here]
        skill = sum(jnp.abs(f - truth) for f in fields) / members
        spread = sum(jnp.abs(fields[j] - fields[k]) for j in range(members) for k in range(j))
        out_ref[here] = skill - (2.0 * coeff) * spread


IN_VMEM = pl.BlockSpec(memory_space=pltpu.VMEM)
ANYWHERE = pl.BlockSpec(memory_space=pl.ANY)
IN_HBM = pl.BlockSpec(memory_space=pltpu.HBM)


def near_by(value):
    return pltpu.with_memory_space_constraint(value, pltpu.VMEM)


def exchange(value, first, lanes):
    pairs = [(i, i + 1) for i in range(first, lanes - 1, 2)]
    return lax.ppermute(value, "mp", pairs + [(j, i) for i, j in pairs])


def project(tokens, gain, w_qkv):
    rows, model = tokens.shape
    steps = 3 * model // STEP_COLS
    return pl.pallas_call(
        functools.partial(project_kernel, model // HEADS),
        in_specs=[IN_HBM] * 3,
        out_specs=[IN_HBM, IN_HBM],
        out_shape=[jax.ShapeDtypeStruct((rows, model), BF16), jax.ShapeDtypeStruct((rows, 2 * model), BF16)],
        scratch_shapes=[
            pltpu.VMEM((rows, model), BF16),
            pltpu.VMEM((1, model), F32),
            pltpu.VMEM((steps, model, STEP_COLS), BF16),
            pltpu.VMEM((steps, rows, STEP_COLS), BF16),
            pltpu.SemaphoreType.DMA,
            pltpu.SemaphoreType.DMA,
            pltpu.SemaphoreType.DMA((steps,)),
            pltpu.SemaphoreType.DMA((steps,)),
        ],
        compiler_params=pltpu.CompilerParams(vmem_limit_bytes=VMEM_LIMIT),
        cost_estimate=LONG,
        name="project",
    )(tokens, w_qkv, gain)


def own_attention(queries, kv):
    rows, model = queries.shape
    pair = 2 * model // HEADS
    pairs = HEADS // 2 - FULL_STEPS * STEP_PAIRS
    held = lambda dtype: pltpu.VMEM((pairs, rows, pair), dtype)
    return pl.pallas_call(
        functools.partial(own_kernel, model // HEADS),
        in_specs=[IN_HBM] * 2,
        out_specs=[IN_HBM] * 3,
        out_shape=[jax.ShapeDtypeStruct((rows, pairs * pair), F32)] * 3,
        scratch_shapes=[held(BF16)] * 3
        + [held(F32)] * 3
        + [pltpu.SemaphoreType.DMA((pairs, 3)), pltpu.SemaphoreType.DMA((pairs, 3))],
        compiler_params=pltpu.CompilerParams(vmem_limit_bytes=SHARED_LIMIT),
        cost_estimate=LONG,
        name="own_tokens",
    )(queries, kv)


def far_attention(
    far, w_qkv, chip_kv, own_kv, queries, sums, totals, tops, w_out, tokens, gain, w_dec, near, edge_weights, dests
):
    rows, model = tokens.shape
    points = near.shape[1]
    span = rows + FAR_ROWS
    steps = HEADS // (2 * STEP_PAIRS)
    held = lambda dtype, cols=model: pltpu.VMEM((rows, cols), dtype)
    return pl.pallas_call(
        functools.partial(far_kernel, model // HEADS),
        in_specs=[IN_HBM] * 7 + [IN_VMEM] * 7,
        out_specs=IN_VMEM,
        out_shape=jax.ShapeDtypeStruct((dests, w_dec.shape[0], points // dests), BF16),
        scratch_shapes=[
            held(BF16), pltpu.VMEM((3 * rows, 2 * model), BF16), held(BF16),
            held(F32, sums.shape[1]), held(F32, sums.shape[1]), held(F32, sums.shape[1]),
            held(BF16, points), held(BF16, points),
            pltpu.VMEM((rows // FAR_ROWS, span, 2 * FAR_ROWS), F32), held(BF16), pltpu.SemaphoreType.DMA,
            pltpu.SemaphoreType.DMA((steps, 6)),
        ],
        compiler_params=pltpu.CompilerParams(vmem_limit_bytes=SHARED_LIMIT),
        cost_estimate=LONG,
        name="neighbour_tokens",
    )(
        far, chip_kv, own_kv, queries, sums, totals, tops,
        *[near_by(a) for a in (w_qkv, w_out, tokens, gain, w_dec, near, edge_weights)],
    )


def one_member(tokens, far, ln_gain, w_qkv, w_out, near, edge_weights, w_dec):
    gain = ln_gain[None]
    queries, kv = project(tokens, gain, w_qkv)
    chip_kv = exchange(kv, 0, lax.axis_size("mp"))
    state = own_attention(queries, kv)
    return far_attention(
        far, w_qkv, chip_kv, kv, queries, *state, w_out, tokens, gain, w_dec, near, edge_weights, lax.axis_size("ens")
    )


def shards(tokens, ln_gain, w_qkv, w_out, neighbours, edge_weights, w_dec, truth):
    far = exchange(tokens, 1, lax.axis_size("mp"))
    decoded = jnp.stack(
        [
            one_member(tokens[m], far[m], ln_gain, w_qkv, w_out, neighbours, edge_weights, w_dec)
            for m in range(tokens.shape[0])
        ]
    )
    gathered = lax.all_to_all(decoded, "ens", split_axis=1, concat_axis=0, tiled=True)
    gathered = gathered.reshape((-1,) + gathered.shape[2:])
    members = gathered.shape[0]
    coeff = ALPHA / (2.0 * members * (members - 1)) + (1.0 - ALPHA) / (2.0 * members * members)
    return pl.pallas_call(
        functools.partial(score_kernel, members, coeff),
        out_shape=jax.ShapeDtypeStruct(truth.shape, F32),
        compiler_params=pltpu.CompilerParams(vmem_limit_bytes=16 * MIB),
        name="scores",
    )(gathered, truth)


def solution(mesh):
    in_specs = (
        P("ens", "mp", None),
        P(),
        P(),
        P(),
        P(None, "mp"),
        P(None, "mp"),
        P(),
        P(None, ("mp", "ens")),
    )
    out_specs = P(None, ("mp", "ens"))
    return jax.shard_map(shards, mesh=mesh, in_specs=in_specs, out_specs=out_specs, check_vma=False)
```
